512 devices in a mesh: section: 8 (over x, core), seq: 64 (over z, y).
Axes of the slice: x: 4, y: 8, z: 8, core: 2. Of those that a mesh axis runs over, the one named last changes fastest.
Arguments:
- llm_grad: bfloat16 [8, 16384, 4096], P('section', 'seq'), may hold values from -6 to 6
- counts: int32 [2, 64], replicated, may hold values from 1 to 20, 1024 in all within a row
- offsets: int32 [2, 64], replicated, may hold values from 0 to 16364, as said below
- owner: int32 [2, 64], replicated, may hold values from 0 to 63, each once within a row
- w_up: bfloat16 [8, 4608, 4608], P('section', 'seq'), as said below
- w_down: bfloat16 [8, 4608, 4096], P('section', 'seq'), as said below
- pre_act: bfloat16 [8, 1280, 4608], P('section', None, 'seq'), may hold values from -6 to 6
- fc1_input: bfloat16 [8, 1280, 4608], P('section', None, 'seq'), may hold values from -6 to 6
- level_input: bfloat16 [8, 1280, 4608], P('section', 'seq'), may hold values from -6 to 6
- ln_gain: float32 [8, 4608], P('section'), may hold values from 0.5 to 1.5, as said below
Outputs:
- vit_grad: bfloat16 [8, 1280, 4608], P('section', 'seq')
- up_grad: bfloat16 [8, 4608, 4608], P('section', 'seq')
- down_grad: bfloat16 [8, 4608, 4096], P('section', 'seq')
The draws below stay inside these ranges and needn't reach their ends.
Inputs may be any that keep to these rules, and one draw needn't show every extreme that they name: Image i lies within the positions of seq device i: i * 256 <= offsets[m, i] <= (i + 1) * 256 - 20. Each micro-batch's counts sum to 1024; in each some image has exactly 20. `owner`: in each micro-batch each seq device holds exactly one image. The micro-batches share the level's weights: w_up[s] depends on s % 4 only. w_down[s] depends on s % 4 only. ln_gain[s] depends on s % 4 only.
All inputs are finite; a program needn't handle non-finite values.
Results may differ from the reference program's by a relative error of at most 0.0057.
Values may be sent and summed in bfloat16 or wider, within the bound.
No kernel may reach another device: no remote copies, remote signals or barrier semaphores. Data moves between devices by JAX's collectives and lax.ppermute only.
A program may use at most 128 MiB of HBM per device.

```python
import math
import jax
import jax.numpy as jnp
import numpy as np
from jax import lax

D_LLM = 4096
MERGE = 4608
LEVELS = 4
MICRO = 2
TOK_DEV = 256
VIS_DEV = 16
SLOT_DEV = 20
IMAGES = 64
TOKENS = 16384
N_SECTION = 8
N_SEQ = 64


def draw_offsets(key, part):
    key = jax.random.fold_in(key, 7)
    jitter = jax.random.randint(key, (MICRO, IMAGES), 0, TOK_DEV - SLOT_DEV + 1)
    return (jnp.arange(IMAGES, dtype=jnp.int32)[None, :] * TOK_DEV + jitter).astype(jnp.int32)


def draw_w_up(key, part):
    key = jax.random.fold_in(key, 11)
    base = jnp.clip(jax.random.normal(key, (LEVELS, MERGE, MERGE), jnp.float32), -6.0, 6.0) * MERGE ** (-0.5)
    return jnp.tile(base, (MICRO, 1, 1)).astype(jnp.bfloat16)


def draw_w_down(key, part):
    key = jax.random.fold_in(key, 13)
    base = jnp.clip(jax.random.normal(key, (LEVELS, MERGE, D_LLM), jnp.float32), -6.0, 6.0) * MERGE ** (-0.5)
    return jnp.tile(base, (MICRO, 1, 1)).astype(jnp.bfloat16)


def draw_ln_gain(key, part):
    key = jax.random.fold_in(key, 17)
    base = jax.random.uniform(key, (LEVELS, MERGE), jnp.float32, 0.5, 1.5)
    return jnp.tile(base, (MICRO, 1)).astype(jnp.float32)


def levels(rng, extent, split, least, top_value):
    def one(axis_at, shards_of):
        heights = jax.random.uniform(jax.random.fold_in(jax.random.fold_in(rng, 6), axis_at), (shards_of,), jnp.float32, least / len(split), top_value / len(split))
        return jnp.repeat(jnp.exp(heights), extent[axis_at] // shards_of).reshape((-1,) + (1,) * (len(extent) - axis_at - 1))

    level = one(*split[0])
    for cut in split[1:]:
        level = level * one(*cut)
    return level


def profile(amount, total, bound, skew):
    portions = [(1 << 20) // math.isqrt(rank ** skew) + 1 for rank in range(2, amount + 1)]
    surplus, given = total - bound - (amount - 1), [1] * (amount - 1)
    while surplus > 0:
        movable = [i for i in range(amount - 1) if given[i] < bound]
        whole, budget = sum([portions[i] for i in movable]), surplus
        for i in movable:
            more = min(bound - given[i], max(1, budget * portions[i] // whole), surplus)
            given[i] = given[i] + more
            surplus = surplus - more
    return np.array([bound] + given)


def uneven_parts(own_key, count, total, limit, skew):
    if count == 2:
        one = jax.random.randint(own_key, (), max(1, total - limit), min(limit, total - 1) + 1)
        return jnp.stack([one, total - one])
    sizes = jnp.asarray(profile(count, total, limit, skew), jnp.int32)
    twos = (count - 1) // 2
    donor, taker = sizes[1:1 + 2 * twos:2], sizes[2:2 + 2 * twos:2]
    margin = jnp.minimum(donor - 1, limit - taker)
    passed = jax.random.randint(jax.random.fold_in(own_key, 1), (twos,), 0, 1 << 20) % (margin + 1)
    sizes = sizes.at[1:1 + 2 * twos:2].set(donor - passed).at[2:2 + 2 * twos:2].set(taker + passed)
    return sizes[jax.random.permutation(jax.random.fold_in(own_key, 2), count)]


def gaussian(key, extent, width, most, split=(), kind=jnp.bfloat16):
    values = jax.random.normal(key, extent, jnp.float32) * width
    if len(split) > 0:
        values = levels(key, extent, split, -0.22, 0.18) * values
    return jnp.clip(values, min=-most, max=most).astype(kind)


def setup_inputs(seed: int = 0) -> dict:
    streams_of = jax.random.split(jax.random.key(seed), 11)
    llm_grad = gaussian(streams_of[0], (N_SECTION, TOKENS, D_LLM), 1.0, 6.0, ((0, 8), (1, 64)))
    counts = jax.vmap(lambda own: uneven_parts(own, IMAGES, VIS_DEV * N_SEQ, SLOT_DEV, 2))(jax.random.split(streams_of[1], MICRO)).reshape((MICRO, IMAGES)).astype(jnp.int32)
    offsets = draw_offsets(jax.random.fold_in(streams_of[10], 71), 0)
    owner = jax.vmap(lambda own: jax.random.permutation(own, IMAGES))(jax.random.split(streams_of[3], MICRO)).reshape((MICRO, IMAGES)).astype(jnp.int32)
    w_up = draw_w_up(jax.random.fold_in(streams_of[10], 71), 0)
    w_down = draw_w_down(jax.random.fold_in(streams_of[10], 71), 0)
    pre_act = gaussian(streams_of[6], (N_SECTION, IMAGES * SLOT_DEV, MERGE), 1.0, 6.0, ((0, 8), (2, 64)))
    fc1_input = gaussian(streams_of[7], (N_SECTION, IMAGES * SLOT_DEV, MERGE), 1.0, 6.0, ((0, 8), (2, 64)))
    level_input = gaussian(streams_of[8], (N_SECTION, N_SEQ * SLOT_DEV, MERGE), 1.0, 6.0, ((0, 8), (1, 64)))
    ln_gain = draw_ln_gain(jax.random.fold_in(streams_of[10], 71), 0)
    return {"llm_grad": llm_grad, "counts": counts, "offsets": offsets, "owner": owner, "w_up": w_up, "w_down": w_down, "pre_act": pre_act, "fc1_input": fc1_input, "level_input": level_input, "ln_gain": ln_gain}


inv_sqrt_two = 0.7071067811865476
inv_sqrt_two_pi = 0.3989422804014327

def gelu_parts(pre_float):
    cdf_part = 0.5 * (1.0 + jax.scipy.special.erf(pre_float * inv_sqrt_two))
    activated = pre_float * cdf_part
    slope = cdf_part + pre_float * jnp.exp(-0.5 * pre_float * pre_float) * inv_sqrt_two_pi
    return (activated, slope)

def norm_backward(level_rows, owned, gain):
    x_float = level_rows.astype(jnp.float32)
    row_mean = lax.optimization_barrier(jnp.mean(x_float, axis=-1, keepdims=True))
    centred = x_float - row_mean
    variance = lax.optimization_barrier(jnp.mean(centred * centred, axis=-1, keepdims=True))
    inv_std = 1.0 / jnp.sqrt(variance + 1e-06)
    normalised = centred * inv_std
    scaled = owned.astype(jnp.float32) * gain[None, :]
    first_mean = lax.optimization_barrier(jnp.mean(scaled, axis=-1, keepdims=True))
    second_mean = lax.optimization_barrier(jnp.mean(scaled * normalised, axis=-1, keepdims=True))
    return inv_std * (scaled - first_mean - normalised * second_mean)

def one_level(llm_rows, counts, offsets, owner, up_weight, down_weight, pre_rows, feed_rows, level_rows, gain):
    slot_iota = jnp.arange(SLOT_DEV, dtype=jnp.int32)
    positions = (offsets[:, None] + slot_iota[None, :]).reshape(-1).astype(jnp.int32)
    live_slot = (slot_iota[None, :] < counts[:, None]).reshape(-1)
    visual = jnp.take(llm_rows, positions, axis=0)
    visual = jnp.where(live_slot[:, None], visual, jnp.zeros_like(visual))
    activated, slope = gelu_parts(pre_rows.astype(jnp.float32))
    hidden_rows = activated.astype(jnp.bfloat16)
    grad_hidden = jnp.dot(visual, down_weight.T, preferred_element_type=jnp.float32)
    down_grad = jnp.dot(hidden_rows.T, visual, preferred_element_type=jnp.float32).astype(jnp.bfloat16)
    grad_pre = (grad_hidden * slope).astype(jnp.bfloat16)
    grad_in = jnp.dot(grad_pre, up_weight.T, preferred_element_type=jnp.float32).astype(jnp.bfloat16)
    up_grad = jnp.dot(feed_rows.T, grad_pre, preferred_element_type=jnp.float32).astype(jnp.bfloat16)
    count_images = counts.shape[0]
    inverse = jnp.zeros((count_images,), jnp.int32).at[owner].set(jnp.arange(count_images, dtype=jnp.int32))
    owned = grad_in.reshape(count_images, SLOT_DEV, MERGE)[inverse].reshape(-1, MERGE)
    level_part = norm_backward(level_rows, owned, gain)
    return (level_part, up_grad, down_grad)

def reference(llm_grad, counts, offsets, owner, w_up, w_down, pre_act, fc1_input, level_input, ln_gain):
    parts = []
    up_list = []
    down_list = []
    for entry in range(N_SECTION):
        micro = entry // LEVELS
        level_part, up_grad, down_grad = one_level(llm_grad[entry], counts[micro], offsets[micro], owner[micro], w_up[entry], w_down[entry], pre_act[entry], fc1_input[entry], level_input[entry], ln_gain[entry])
        parts.append(level_part)
        up_list.append(up_grad)
        down_list.append(down_grad)
    summed = jnp.zeros_like(parts[0])
    carried = [None] * N_SECTION
    for entry in range(N_SECTION - 1, -1, -1):
        if entry % LEVELS == LEVELS - 1:
            summed = jnp.zeros_like(parts[0])
        summed = parts[entry] + summed
        carried[entry] = summed.astype(jnp.bfloat16)
    return (jnp.stack(carried), jnp.stack(up_list), jnp.stack(down_list))
```

```python
import jax
import jax.numpy as jnp
from jax import lax
from jax.sharding import Mesh, PartitionSpec as P

inv_sqrt_two = 0.7071067811865476
inv_sqrt_two_pi = 0.3989422804014327
f32 = jnp.float32
bf16 = jnp.bfloat16

SIDE = 8
LEVELS = 4
MAIN = 16
REST = 4


def gelu_parts(pre_float):
    cdf_part = 0.5 * (1.0 + jax.scipy.special.erf(pre_float * inv_sqrt_two))
    activated = pre_float * cdf_part
    slope = cdf_part + pre_float * jnp.exp(-0.5 * pre_float * pre_float) * inv_sqrt_two_pi
    return (activated, slope)


def norm_backward(level_rows, owned, gain):
    x_float = level_rows.astype(f32)
    row_mean = jnp.mean(x_float, axis=-1, keepdims=True)
    centred = x_float - row_mean
    variance = jnp.mean(centred * centred, axis=-1, keepdims=True)
    inv_std = 1.0 / jnp.sqrt(variance + 1e-06)
    normalised = centred * inv_std
    scaled = owned.astype(f32) * gain[None, :]
    first_mean = jnp.mean(scaled, axis=-1, keepdims=True)
    second_mean = jnp.mean(scaled * normalised, axis=-1, keepdims=True)
    return inv_std * (scaled - first_mean - normalised * second_mean)


def dot(a, b, dims):
    return lax.dot_general(a, b, (dims, ((), ())), preferred_element_type=f32)


def body(llm_grad, counts, offsets, owner, w_up, w_down, pre_act, fc1_input, level_input, ln_gain):
    z_index = lax.axis_index("z")
    y_index = lax.axis_index("y")
    device_index = z_index * SIDE + y_index
    section_index = lax.axis_index("section")
    micro_index = section_index // LEVELS
    level_index = section_index % LEVELS
    counts_row = lax.dynamic_index_in_dim(counts, micro_index, 0, keepdims=False)
    offsets_row = lax.dynamic_index_in_dim(offsets, micro_index, 0, keepdims=False)
    owner_row = lax.dynamic_index_in_dim(owner, micro_index, 0, keepdims=False)
    tok_count, width = llm_grad.shape[1:]
    slots = level_input.shape[1]
    images = counts.shape[1]
    rows = images * slots
    own = w_up.shape[1]
    merge = w_up.shape[2]
    chunk = width // REST
    main_rows = images * MAIN

    start_row = offsets_row[device_index] - device_index * tok_count
    window = lax.dynamic_slice_in_dim(llm_grad[0], start_row, slots, 0)
    live = jnp.arange(slots, dtype=jnp.int32) < counts_row[device_index]
    visual = jnp.where(live[:, None], window, jnp.zeros_like(window))
    tail = visual[MAIN:].reshape(REST, REST, chunk).transpose(1, 0, 2).reshape(MAIN, chunk)
    shard = jnp.concatenate([visual[:MAIN], tail], axis=1)
    gathered = lax.all_gather(shard, ("z", "y"), axis=0, tiled=True)

    owner_base = ((owner_row % SIDE) * SIDE + owner_row // SIDE) * slots
    place = owner_base[:, None] + jnp.arange(slots, dtype=jnp.int32)[None, :]
    image_place = place.reshape(rows)
    split_place = jnp.concatenate([place[:, :MAIN].reshape(-1), place[:, MAIN:].reshape(-1)])
    columns = jnp.arange(rows, dtype=jnp.int32)[None, :]
    image_to_owner = (image_place[:, None] == columns).astype(bf16)
    split_to_owner = (split_place[:, None] == columns).astype(bf16)

    weight = w_up[0].reshape(own, SIDE, SIDE, own).transpose(2, 0, 1, 3).reshape(SIDE, own, SIDE * own)
    weight = lax.all_to_all(weight, "y", split_axis=0, concat_axis=0).reshape(SIDE * own, SIDE * own)
    feed = dot(fc1_input[0], image_to_owner, ((0,), (0,))).astype(bf16)
    feed = lax.all_to_all(jnp.broadcast_to(feed[None], (SIDE, own, rows)), "y", split_axis=0, concat_axis=0)
    feed = feed.reshape(SIDE * own, rows)

    pre = pre_act[0].reshape(images, slots, own)
    pre = jnp.concatenate([pre[:, :MAIN].reshape(main_rows, own), pre[:, MAIN:].reshape(images * REST, own)], axis=0)
    activated, slope = gelu_parts(pre.astype(f32))
    activated = activated.astype(bf16)

    down = w_down[0]
    down_chunks = down.reshape(own, REST, chunk).transpose(1, 0, 2).reshape(REST * own, chunk)
    row_chunk = (jnp.arange(main_rows, dtype=jnp.int32) // REST) % REST
    same_chunk = row_chunk[:, None] == jnp.arange(REST * own, dtype=jnp.int32)[None, :] // own

    main_part = gathered[:, :width]
    tail_part = gathered[:, width:]
    hidden_main = dot(main_part, down, ((1,), (1,)))
    hidden_tail = dot(tail_part, down_chunks, ((1,), (1,)))
    hidden_tail = jnp.where(same_chunk, hidden_tail, 0.0).reshape(images, REST, REST, REST, own)
    hidden_tail = hidden_tail.sum(axis=(1, 3)).reshape(images * REST, own)
    grad_hidden = jnp.concatenate([hidden_main, hidden_tail], axis=0)
    grad_pre = (grad_hidden * slope).astype(bf16)
    grad_pre = dot(grad_pre, split_to_owner, ((0,), (0,))).astype(bf16)
    panel = lax.all_gather(grad_pre, "z", axis=0, tiled=True)

    act_tail = activated[main_rows:].reshape(images, 1, REST, 1, own)
    act_tail = jnp.broadcast_to(act_tail, (images, REST, REST, REST, own)).reshape(main_rows, REST * own)
    act_tail = jnp.where(same_chunk, act_tail, jnp.zeros_like(act_tail))
    grad_down = dot(activated[:main_rows], main_part, ((0,), (0,)))
    grad_down_tail = dot(act_tail, tail_part, ((0,), (0,)))
    grad_down_tail = grad_down_tail.reshape(REST, own, chunk).transpose(1, 0, 2).reshape(own, width)
    grad_down = (grad_down + grad_down_tail).astype(bf16)

    grad_in = dot(panel, weight, ((0,), (1,))).astype(bf16)
    grad_in = lax.psum_scatter(grad_in, "y", scatter_dimension=0, tiled=True)
    grad_up = dot(feed, panel, ((1,), (1,))).astype(bf16).reshape(SIDE, own, SIDE * own)
    grad_up = lax.all_to_all(grad_up, "y", split_axis=0, concat_axis=0)
    grad_up = grad_up.reshape(SIDE, own, SIDE, own).transpose(1, 2, 0, 3).reshape(own, merge)

    owned = lax.all_to_all(grad_in.reshape(SIDE, slots, SIDE * own), "z", split_axis=0, concat_axis=0)
    owned = owned.transpose(1, 0, 2).reshape(slots, merge)
    level_part = norm_backward(level_input[0], owned, ln_gain[0])
    is_top = level_index == LEVELS - 1
    summed = level_part
    count = lax.axis_size("section")
    for hop in range(LEVELS - 1):
        incoming = lax.ppermute(summed, "section", [(source, source - 1) for source in range(1, count)])
        summed = level_part + jnp.where(is_top, jnp.zeros_like(incoming), incoming)
    return (summed.astype(bf16)[None], grad_up[None], grad_down[None])


def solution(mesh):
    sections = mesh.devices.shape[0]
    cube = Mesh(mesh.devices.reshape(sections, SIDE, SIDE), ("section", "z", "y"))
    rows = P("section", ("z", "y"), None)
    cols = P("section", None, ("z", "y"))
    return jax.shard_map(
        body,
        mesh=cube,
        in_specs=(rows, P(), P(), P(), rows, rows, cols, cols, rows, P("section", None)),
        out_specs=(rows, rows, rows),
        check_vma=False,
    )
```

```python
import jax
import jax.numpy as jnp
from jax import lax
from jax.experimental import pallas as pl
from jax.experimental.pallas import tpu as pltpu
from jax.sharding import Mesh, PartitionSpec as P

inv_sqrt_two = 0.7071067811865476
inv_sqrt_two_pi = 0.3989422804014327
f32 = jnp.float32
bf16 = jnp.bfloat16

SIDE = 8
LEVELS = 4
MAIN = 16
REST = 4
LANES = 128
STEP = 512
VMEM_BYTES = 48 * 1024 * 1024


def gelu_parts(pre_float):
    cdf_part = 0.5 * (1.0 + jax.scipy.special.erf(pre_float * inv_sqrt_two))
    activated = pre_float * cdf_part
    slope = cdf_part + pre_float * jnp.exp(-0.5 * pre_float * pre_float) * inv_sqrt_two_pi
    return (activated, slope)


def norm_backward(level_rows, owned, gain):
    x_float = level_rows.astype(f32)
    row_mean = jnp.mean(x_float, axis=-1, keepdims=True)
    centred = x_float - row_mean
    variance = jnp.mean(centred * centred, axis=-1, keepdims=True)
    inv_std = 1.0 / jnp.sqrt(variance + 1e-06)
    normalised = centred * inv_std
    scaled = owned.astype(f32) * gain[None, :]
    first_mean = jnp.mean(scaled, axis=-1, keepdims=True)
    second_mean = jnp.mean(scaled * normalised, axis=-1, keepdims=True)
    return inv_std * (scaled - first_mean - normalised * second_mean)


def dot(a, b, dims):
    return lax.dot_general(a, b, (dims, ((), ())), preferred_element_type=f32)


def shard_kernel(info_ref, first_ref, second_ref, third_ref, out_ref):
    delta = info_ref[1]
    count = info_ref[2]
    width = first_ref.shape[1]
    chunk = width // REST
    block = jnp.concatenate(
        [first_ref[...].astype(f32), second_ref[...].astype(f32), third_ref[...].astype(f32)], axis=0
    )
    total = block.shape[0]
    block = pltpu.roll(block, lax.rem(total - delta, total), 0)[: MAIN + 2 * REST]
    slot = lax.broadcasted_iota(jnp.int32, block.shape, 0)
    block = jnp.where(slot < count, block, 0.0)
    out_ref[:, :width] = block[:MAIN].astype(bf16)
    pieces = [block[MAIN:, c * chunk : (c + 1) * chunk] for c in range(REST)]
    upper = pieces[0] + pltpu.roll(pieces[1], REST, 0)
    lower = pieces[2] + pltpu.roll(pieces[3], REST, 0)
    out_ref[:, width:] = jnp.concatenate([upper, lower], axis=0).astype(bf16)


def image_shard(rows, start, count):
    tok_count, width = rows.shape
    base = jnp.minimum(start // MAIN, tok_count // MAIN - 3)
    info = jnp.stack([base, start - base * MAIN, count]).astype(jnp.int32)
    out_cols = width + width // REST

    def at(ahead):
        return pl.BlockSpec((MAIN, width), lambda step, info_ref: (info_ref[0] + ahead, 0))

    return pl.pallas_call(
        shard_kernel,
        grid_spec=pltpu.PrefetchScalarGridSpec(
            num_scalar_prefetch=1,
            grid=(1,),
            in_specs=[at(0), at(1), at(2)],
            out_specs=pl.BlockSpec((MAIN, out_cols), lambda step, info_ref: (0, 0)),
        ),
        out_shape=jax.ShapeDtypeStruct((MAIN, out_cols), bf16),
        compiler_params=pltpu.CompilerParams(vmem_limit_bytes=VMEM_BYTES),
    )(info, rows, rows, rows)


def hidden_kernel(main_steps, source_ref, block_ref, main_ref, tail_ref, main_slope_ref, tail_slope_ref, out_ref,
                  main_sum, tail_sum, order):
    step = pl.program_id(0)
    contract = (((1,), (1,)), ((), ()))

    @pl.when(step == 0)
    def _():
        main_sum[...] = jnp.zeros_like(main_sum)
        tail_sum[...] = jnp.zeros_like(tail_sum)

    part = source_ref.shape[0]
    index = lax.broadcasted_iota(jnp.int32, (part, order.shape[1]), 1)
    at = pl.ds(pl.multiple_of(step * part, part), part)
    order[at, :] = jnp.where(index == source_ref[...], 1.0, 0.0).astype(bf16)

    @pl.when(step < main_steps)
    def _():
        main_sum[...] += lax.dot_general(block_ref[...], main_ref[...], contract, preferred_element_type=f32)

    @pl.when(step >= main_steps)
    def _():
        tail_sum[...] += lax.dot_general(block_ref[...], tail_ref[...], contract, preferred_element_type=f32)

    @pl.when(step == pl.num_programs(0) - 1)
    def _():
        rows = main_sum.shape[0]
        main = (main_sum[...] * main_slope_ref[...]).astype(bf16)
        row = lax.broadcasted_iota(jnp.int32, (rows, LANES), 0)
        chunk = lax.rem(lax.div(row, REST), REST)
        tail = jnp.zeros((rows, LANES), f32)
        for c in range(REST):
            tail += jnp.where(chunk == c, tail_sum[:, c * LANES : (c + 1) * LANES], 0.0)
        tail = tail.reshape(rows // MAIN, 2, 2 * REST, LANES)
        tail = (tail[:, 0] + tail[:, 1]).reshape(rows // 2, LANES)
        tail = tail + pltpu.roll(tail, rows // 2 - REST, 0)
        tail = (tail * tail_slope_ref[...]).astype(bf16)
        result = jnp.dot(order[:, :rows], main, preferred_element_type=f32)
        result += jnp.dot(order[:, rows:], tail, preferred_element_type=f32)
        out_ref[...] = result.T[: out_ref.shape[0]].astype(bf16)


def hidden_gradient(gathered, down, slope, inverse):
    main_rows, cols = gathered.shape
    own, width = down.shape
    images, slots = slope.shape[:2]
    chunk = width // REST
    rows = images * slots
    steps, main_steps = cols // STEP, width // STEP
    pad = LANES - own
    main_weight = jnp.pad(down, ((0, pad), (0, 0)))
    tail_weight = main_weight.reshape(LANES, REST, chunk).transpose(1, 0, 2).reshape(REST * LANES, chunk)
    main_slope = jnp.pad(slope[:, :MAIN].reshape(main_rows, own), ((0, 0), (0, pad)))
    tail_slope = jnp.pad(slope[:, MAIN:], ((0, 0), (0, REST), (0, pad))).reshape(main_rows // 2, LANES)
    slot = jnp.arange(slots, dtype=jnp.int32)[None, :]
    image = inverse.reshape(SIDE, SIDE).T.reshape(images, 1)
    source = jnp.where(slot < MAIN, image * MAIN + slot, main_rows + image * 2 * REST + slot - MAIN)
    source = source.reshape(rows, 1).astype(jnp.int32)
    main_weight, tail_weight, main_slope, tail_slope, source, gathered = lax.optimization_barrier(
        (main_weight, tail_weight, main_slope, tail_slope, source, gathered)
    )
    whole = lambda step: (0, 0)
    return pl.pallas_call(
        lambda *refs: hidden_kernel(main_steps, *refs),
        grid=(steps,),
        in_specs=[
            pl.BlockSpec((rows // steps, 1), lambda step: (step, 0)),
            pl.BlockSpec((main_rows, STEP), lambda step: (0, step)),
            pl.BlockSpec((LANES, STEP), lambda step: (0, jnp.minimum(step, main_steps - 1))),
            pl.BlockSpec((REST * LANES, STEP), lambda step: (0, jnp.maximum(step - main_steps, 0))),
            pl.BlockSpec((main_rows, LANES), whole),
            pl.BlockSpec((main_rows // 2, LANES), whole),
        ],
        out_specs=pl.BlockSpec((own, rows), whole),
        out_shape=jax.ShapeDtypeStruct((own, rows), bf16),
        scratch_shapes=[
            pltpu.VMEM((main_rows, LANES), f32),
            pltpu.VMEM((main_rows, REST * LANES), f32),
            pltpu.VMEM((rows, main_rows + main_rows // 2), bf16),
        ],
        compiler_params=pltpu.CompilerParams(vmem_limit_bytes=VMEM_BYTES),
    )(source, gathered, main_weight, tail_weight, main_slope, tail_slope)


def body(llm_grad, counts, offsets, owner, w_up, w_down, pre_act, fc1_input, level_input, ln_gain):
    z_index = lax.axis_index("z")
    y_index = lax.axis_index("y")
    device_index = z_index * SIDE + y_index
    section_index = lax.axis_index("section")
    micro_index = section_index // LEVELS
    level_index = section_index % LEVELS
    tok_count, width = llm_grad.shape[1:]
    slots = level_input.shape[1]
    images = counts.shape[1]
    rows = images * slots
    own = w_up.shape[1]
    merge = w_up.shape[2]
    chunk = width // REST
    main_rows = images * MAIN

    start_row = offsets[micro_index, device_index] - device_index * tok_count
    shard = image_shard(llm_grad[0], start_row, counts[micro_index, device_index])
    gathered = lax.all_gather(shard, ("z", "y"), axis=0, tiled=True)

    owner_row = lax.dynamic_index_in_dim(owner, micro_index, 0, keepdims=False)
    number = jnp.arange(images, dtype=jnp.int32)
    inverse = jnp.sum(jnp.where(owner_row[None, :] == number[:, None], number[None, :], 0), axis=1)
    owner_base = ((owner_row % SIDE) * SIDE + owner_row // SIDE) * slots
    place = (owner_base[:, None] + jnp.arange(slots, dtype=jnp.int32)[None, :]).reshape(rows)
    to_owner = (place[:, None] == jnp.arange(rows, dtype=jnp.int32)[None, :]).astype(bf16)

    weight = w_up[0].reshape(own, SIDE, SIDE, own).transpose(2, 0, 1, 3).reshape(SIDE, own, SIDE * own)
    weight = lax.all_to_all(weight, "y", split_axis=0, concat_axis=0).reshape(SIDE * own, SIDE * own)
    feed = dot(fc1_input[0], to_owner, ((0,), (0,))).astype(bf16)
    feed = jnp.broadcast_to(feed[None], (SIDE, own, rows))
    activated, slope = gelu_parts(pre_act[0].astype(f32).reshape(images, slots, own))
    activated = activated.astype(bf16)
    row_chunk = (jnp.arange(main_rows, dtype=jnp.int32) // REST) % REST
    same_chunk = row_chunk[:, None] == jnp.arange(REST * own, dtype=jnp.int32)[None, :] // own
    act_main = activated[:, :MAIN].reshape(main_rows, own)
    act_tail = jnp.broadcast_to(activated[:, None, MAIN:, None, :], (images, REST, REST, REST, own))
    act_tail = act_tail.reshape(main_rows, REST * own)
    act_tail = jnp.where(same_chunk, act_tail, jnp.zeros_like(act_tail))
    gathered, weight, feed, act_main, act_tail, slope = lax.optimization_barrier(
        (gathered, weight, feed, act_main, act_tail, slope)
    )

    grad_pre = hidden_gradient(gathered, w_down[0], slope, inverse)
    panel = lax.all_gather(grad_pre, "z", axis=0, tiled=True)
    feed = lax.all_to_all(feed, "y", split_axis=0, concat_axis=0).reshape(SIDE * own, rows)
    panel, feed = lax.optimization_barrier((panel, feed))

    grad_in = dot(panel, weight, ((0,), (1,))).astype(bf16)
    grad_in = lax.psum_scatter(grad_in, "y", scatter_dimension=0, tiled=True)
    grad_up = dot(feed, panel, ((1,), (1,))).astype(bf16).reshape(SIDE, own, SIDE * own)
    grad_up = lax.all_to_all(grad_up, "y", split_axis=0, concat_axis=0)
    grad_up = grad_up.reshape(SIDE, own, SIDE, own).transpose(1, 2, 0, 3).reshape(own, merge)
    grad_in, grad_up = lax.optimization_barrier((grad_in, grad_up))
    owned = lax.all_to_all(grad_in.reshape(SIDE, slots, SIDE * own), "z", split_axis=0, concat_axis=0)

    grad_down = dot(act_main, gathered[:, :width], ((0,), (0,)))
    grad_down_tail = dot(act_tail, gathered[:, width:], ((0,), (0,)))
    grad_down_tail = grad_down_tail.reshape(REST, own, chunk).transpose(1, 0, 2).reshape(own, width)
    grad_down = (grad_down + grad_down_tail).astype(bf16)
    owned, grad_down = lax.optimization_barrier((owned, grad_down))

    owned = owned.transpose(1, 0, 2).reshape(slots, merge)
    level_part = norm_backward(level_input[0], owned, ln_gain[0])

    count = lax.axis_size("section")
    other = lax.ppermute(level_part, "section", [(source, source ^ 1) for source in range(count)])
    pair_sum = level_part + other
    below = [(source, source - 2) for source in range(count) if source % LEVELS >= 2]
    above = lax.ppermute(pair_sum.astype(bf16), "section", below).astype(f32)
    summed = jnp.where(level_index % 2 == 0, pair_sum, level_part)
    summed = summed + jnp.where(level_index < 2, above, 0.0)
    return (summed.astype(bf16)[None], grad_up[None], grad_down[None])


def solution(mesh):
    sections = mesh.devices.shape[0]
    cube = Mesh(mesh.devices.reshape(sections, SIDE, SIDE), ("section", "z", "y"))
    rows = P("section", ("z", "y"), None)
    cols = P("section", None, ("z", "y"))
    return jax.shard_map(
        body,
        mesh=cube,
        in_specs=(rows, P(), P(), P(), rows, rows, cols, cols, rows, P("section", None)),
        out_specs=(rows, rows, rows),
        check_vma=False,
    )
```

```python
import jax
import jax.numpy as jnp
from jax import lax
from jax.experimental import pallas as pl
from jax.experimental.pallas import tpu as pltpu
from jax.sharding import Mesh, PartitionSpec as P

inv_sqrt_two = 0.7071067811865476
inv_sqrt_two_pi = 0.3989422804014327
f32 = jnp.float32
bf16 = jnp.bfloat16
f16 = jnp.float16

SIDE = 8
LEVELS = 4
MAIN = 16
REST = 4
LANES = 128
VMEM_BYTES = 48 * 1024 * 1024
FULL = 32768.0
LEAST_POWER = -113
POWERS = (86, 64, 32, 16, 8, 4, 2, 1)


def gelu_parts(pre_float):
    cdf_part = 0.5 * (1.0 + jax.scipy.special.erf(pre_float * inv_sqrt_two))
    activated = pre_float * cdf_part
    slope = cdf_part + pre_float * jnp.exp(-0.5 * pre_float * pre_float) * inv_sqrt_two_pi
    return (activated, slope)


def norm_backward(level_rows, owned, gain):
    x_float = level_rows.astype(f32)
    row_mean = jnp.mean(x_float, axis=-1, keepdims=True)
    centred = x_float - row_mean
    variance = jnp.mean(centred * centred, axis=-1, keepdims=True)
    inv_std = 1.0 / jnp.sqrt(variance + 1e-06)
    normalised = centred * inv_std
    scaled = owned.astype(f32) * gain[None, :]
    first_mean = jnp.mean(scaled, axis=-1, keepdims=True)
    second_mean = jnp.mean(scaled * normalised, axis=-1, keepdims=True)
    return inv_std * (scaled - first_mean - normalised * second_mean)


def dot(a, b, dims):
    return lax.dot_general(a, b, (dims, ((), ())), preferred_element_type=f32)


def block_power(block):
    largest = jnp.max(jnp.abs(block), axis=(0, 1), keepdims=True)
    scale = jnp.full_like(largest, 2.0**LEAST_POWER)
    power = jnp.full_like(largest, float(LEAST_POWER))
    for step in POWERS:
        fits = largest * (scale * 2.0**step) <= FULL
        scale = jnp.where(fits, scale * 2.0**step, scale)
        power = jnp.where(fits, power + float(step), power)
    return scale, power


def shard_kernel(info_ref, counts_ref, offsets_ref, first_ref, second_ref, third_ref, out_ref):
    micro, device = info_ref[0], info_ref[1]
    tok_count = info_ref[2]
    start = offsets_ref[micro, device] - device * tok_count
    delta = start - jnp.minimum(lax.div(start, MAIN), lax.div(tok_count, MAIN) - 3) * MAIN
    count = counts_ref[micro, device]
    width = first_ref.shape[1]
    chunk = width // REST
    block = jnp.concatenate(
        [first_ref[...].astype(f32), second_ref[...].astype(f32), third_ref[...].astype(f32)], axis=0
    )
    total = block.shape[0]
    block = pltpu.roll(block, lax.rem(total - delta, total), 0)[: MAIN + 2 * REST]
    slot = lax.broadcasted_iota(jnp.int32, block.shape, 0)
    block = jnp.where(slot < count, block, 0.0)
    scale, power = block_power(block)
    block = block * scale
    out_ref[:, :width] = block[:MAIN].astype(bf16)
    pieces = [block[MAIN:, c * chunk : (c + 1) * chunk] for c in range(REST)]
    upper = pieces[0] + pltpu.roll(pieces[1], REST, 0)
    lower = pieces[2] + pltpu.roll(pieces[3], REST, 0)
    out_ref[:, width : width + chunk] = jnp.concatenate([upper, lower], axis=0).astype(bf16)
    out_ref[:, width + chunk :] = jnp.broadcast_to(power, (MAIN, LANES)).astype(bf16)


def image_shard(rows, micro, device, counts, offsets):
    tok_count, width = rows.shape
    info = jnp.stack([micro, device, jnp.int32(tok_count)]).astype(jnp.int32)
    out_cols = width + width // REST + LANES

    def at(ahead):
        def index(step, info_ref, counts_ref, offsets_ref):
            start = offsets_ref[info_ref[0], info_ref[1]] - info_ref[1] * tok_count
            return (jnp.minimum(lax.div(start, MAIN), tok_count // MAIN - 3) + ahead, 0)

        return pl.BlockSpec((MAIN, width), index)

    return pl.pallas_call(
        shard_kernel,
        grid_spec=pltpu.PrefetchScalarGridSpec(
            num_scalar_prefetch=3,
            grid=(1,),
            in_specs=[at(0), at(1), at(2)],
            out_specs=pl.BlockSpec((MAIN, out_cols), lambda step, *refs: (0, 0)),
        ),
        out_shape=jax.ShapeDtypeStruct((MAIN, out_cols), bf16),
        compiler_params=pltpu.CompilerParams(vmem_limit_bytes=VMEM_BYTES),
    )(info, counts, offsets, rows, rows, rows)


def hidden_kernel(source_ref, power_ref, main_ref, tail_ref, slope_ref, out_ref, image_rows):
    main_rows, own = main_ref.shape
    rows = image_rows.shape[0]
    images = main_rows // MAIN
    slots = rows // images
    unscale = jnp.exp2(-power_ref[...])
    row = lax.broadcasted_iota(jnp.int32, (main_rows, LANES), 0)
    chunk = lax.rem(lax.div(row, REST), REST)
    tail = jnp.zeros((main_rows, LANES), f32)
    for c in range(REST):
        tail += jnp.where(chunk == c, tail_ref[:, c * LANES : (c + 1) * LANES], 0.0)
    tail = (tail * unscale).reshape(images, 2, 2 * REST, LANES)
    tail = (tail[:, 0] + tail[:, 1]).reshape(main_rows // 2, LANES)
    tail = tail + pltpu.roll(tail, main_rows // 2 - REST, 0)
    main = main_ref[...] * unscale[:, :own]
    image_rows[...] = jnp.zeros_like(image_rows)
    for i in range(images):
        image_rows[i * slots : i * slots + MAIN, :own] = main[i * MAIN : (i + 1) * MAIN]
        image_rows[i * slots + MAIN : (i + 1) * slots, :] = tail[i * 2 * REST : i * 2 * REST + REST]
    grad_pre = (image_rows[:, :own] * slope_ref[...]).astype(bf16)
    scale, power = block_power(grad_pre.astype(f32))
    index = lax.broadcasted_iota(jnp.int32, (LANES, rows), 1)
    for part in range(rows // LANES):
        at = slice(part * LANES, (part + 1) * LANES)
        order = jnp.where(index == source_ref[at, :], 1.0, 0.0).astype(bf16)
        image_rows[at, :own] = jnp.dot(order, grad_pre, preferred_element_type=f32) * scale
    out_ref[:, :rows] = image_rows[...].T[:own].astype(bf16)
    out_ref[:, rows:] = jnp.broadcast_to(power, (own, LANES)).astype(bf16)


def hidden_gradient(source, power, main, tail, slope):
    rows, own = slope.shape
    return pl.pallas_call(
        hidden_kernel,
        out_shape=jax.ShapeDtypeStruct((own, rows + LANES), bf16),
        scratch_shapes=[pltpu.VMEM((rows, LANES), f32)],
        compiler_params=pltpu.CompilerParams(vmem_limit_bytes=VMEM_BYTES),
    )(source, power, main, tail, slope)


def body(llm_grad, counts, offsets, owner, w_up, w_down, pre_act, fc1_input, level_input, ln_gain):
    z_index = lax.axis_index("z")
    y_index = lax.axis_index("y")
    device_index = z_index * SIDE + y_index
    section_index = lax.axis_index("section")
    micro_index = section_index // LEVELS
    level_index = section_index % LEVELS
    tok_count, width = llm_grad.shape[1:]
    slots = level_input.shape[1]
    images = counts.shape[1]
    rows = images * slots
    own = w_up.shape[1]
    merge = w_up.shape[2]
    chunk = width // REST
    main_rows = images * MAIN

    shard = image_shard(llm_grad[0], micro_index, device_index, counts, offsets)
    gathered = lax.all_gather(shard.astype(f16), ("z", "y"), axis=0, tiled=True)
    feed = lax.all_gather(fc1_input[0].T, "z", axis=0, tiled=True)

    owner_row = lax.dynamic_index_in_dim(owner, micro_index, 0, keepdims=False)
    number = jnp.arange(images, dtype=jnp.int32)
    slot = jnp.arange(slots, dtype=jnp.int32)[None, :]
    inverse = jnp.sum(jnp.where(owner_row[None, :] == number[:, None], number[None, :], 0), axis=1)
    source = (inverse[:, None] * slots + slot).reshape(rows, 1).astype(jnp.int32)
    place = (owner_row[:, None] * slots + slot).reshape(rows)

    pre = pre_act[0].astype(f32)
    slope = gelu_parts(pre)[1]
    down = w_down[0]
    tail_weight = jnp.pad(down.reshape(own, REST, chunk), ((0, LANES - own), (0, 0), (0, 0)))
    tail_weight = tail_weight.transpose(1, 0, 2).reshape(REST * LANES, chunk)
    gathered, feed, slope, source, tail_weight = lax.optimization_barrier(
        (gathered, feed, slope, source, tail_weight)
    )

    power = gathered[:, width + chunk :].astype(f32)
    hidden_main = dot(gathered[:, :width].astype(bf16), down, ((1,), (1,)))
    hidden_tail = dot(gathered[:, width : width + chunk].astype(bf16), tail_weight, ((1,), (1,)))
    grad_pre = hidden_gradient(source, power, hidden_main, hidden_tail, slope)
    panel = lax.all_gather(grad_pre.astype(f16), "y", axis=0, tiled=True)
    weight = w_up[0].reshape(own, SIDE, SIDE * own).transpose(1, 0, 2)
    weight = lax.all_to_all(weight, "z", split_axis=0, concat_axis=0).reshape(SIDE * own, SIDE * own)
    panel, weight = lax.optimization_barrier((panel, weight))
    panel = (panel[:, :rows].astype(f32) * jnp.exp2(-panel[:, rows : rows + 1].astype(f32))).astype(bf16)

    grad_in = dot(panel, weight, ((0,), (1,))).astype(bf16)
    grad_in = lax.psum_scatter(grad_in, "z", scatter_dimension=0, tiled=True)

    to_owner = (place[:, None] == jnp.arange(rows, dtype=jnp.int32)[None, :]).astype(bf16)
    feed = dot(feed, to_owner, ((1,), (0,))).astype(bf16)
    grad_up = dot(feed, panel, ((1,), (1,))).astype(bf16).reshape(SIDE, own, SIDE * own)
    grad_up = lax.all_to_all(grad_up, "z", split_axis=0, concat_axis=0)
    grad_up = grad_up.transpose(1, 0, 2).reshape(own, merge)

    unscale = jnp.exp2(-power[:, :1])
    activated = gelu_parts(pre)[0].astype(bf16).reshape(images, slots, own)
    row_chunk = (jnp.arange(main_rows, dtype=jnp.int32) // REST) % REST
    same_chunk = row_chunk[:, None] == jnp.arange(REST * own, dtype=jnp.int32)[None, :] // own
    act_main = (activated[:, :MAIN].reshape(main_rows, own).astype(f32) * unscale).astype(bf16)
    act_tail = jnp.broadcast_to(activated[:, None, MAIN:, None, :], (images, REST, REST, REST, own))
    act_tail = act_tail.reshape(main_rows, REST * own).astype(f32) * unscale
    act_tail = jnp.where(same_chunk, act_tail, 0.0).astype(bf16)
    grad_down = dot(act_main, gathered[:, :width].astype(bf16), ((0,), (0,)))
    grad_down_tail = dot(act_tail, gathered[:, width : width + chunk].astype(bf16), ((0,), (0,)))
    grad_down_tail = grad_down_tail.reshape(REST, own, chunk).transpose(1, 0, 2).reshape(own, width)
    grad_down = (grad_down + grad_down_tail).astype(bf16)
    grad_in, grad_up, grad_down = lax.optimization_barrier((grad_in, grad_up, grad_down))

    owned = lax.all_to_all(grad_in.reshape(SIDE, slots, SIDE * own), "y", split_axis=0, concat_axis=0)
    owned = owned.reshape(SIDE, slots, SIDE, own).transpose(1, 2, 0, 3).reshape(slots, merge)
    level_part = norm_backward(level_input[0], owned, ln_gain[0])

    count = lax.axis_size("section")
    other = lax.ppermute(level_part, "section", [(source, source ^ 1) for source in range(count)])
    pair_sum = level_part + other
    below = [(source, source - 2) for source in range(count) if source % LEVELS >= 2]
    above = lax.ppermute(pair_sum.astype(bf16), "section", below).astype(f32)
    summed = jnp.where(level_index % 2 == 0, pair_sum, level_part)
    summed = summed + jnp.where(level_index < 2, above, 0.0)
    return (summed.astype(bf16)[None], grad_up[None], grad_down[None])


def solution(mesh):
    sections = mesh.devices.shape[0]
    cube = Mesh(mesh.devices.reshape(sections, SIDE, SIDE), ("section", "z", "y"))
    rows = P("section", ("z", "y"), None)
    cols = P("section", None, ("z", "y"))
    return jax.shard_map(
        body,
        mesh=cube,
        in_specs=(rows, P(), P(), P(), rows, rows, cols, cols, rows, P("section", None)),
        out_specs=(rows, rows, rows),
        check_vma=False,
    )
```

```python
import functools

import jax
import jax.numpy as jnp
from jax import lax
from jax.experimental import pallas as pl
from jax.experimental.pallas import tpu as pltpu
from jax.sharding import Mesh, PartitionSpec as P

inv_sqrt_two = 0.7071067811865476
inv_sqrt_two_pi = 0.3989422804014327
f32 = jnp.float32
bf16 = jnp.bfloat16
f16 = jnp.float16

SIDE = 8
LEVELS = 4
MAIN = 16
REST = 4
LANES = 128
VMEM_BYTES = 20 * 1024 * 1024
FULL = 32768.0
LEAST_POWER = -113
POWERS = (86, 64, 32, 16, 8, 4, 2, 1)


def gelu_parts(pre_float):
    cdf_part = 0.5 * (1.0 + jax.scipy.special.erf(pre_float * inv_sqrt_two))
    activated = pre_float * cdf_part
    slope = cdf_part + pre_float * jnp.exp(-0.5 * pre_float * pre_float) * inv_sqrt_two_pi
    return (activated, slope)


def norm_backward(level_rows, owned, gain):
    x_float = level_rows.astype(f32)
    row_mean = jnp.mean(x_float, axis=-1, keepdims=True)
    centred = x_float - row_mean
    variance = jnp.mean(centred * centred, axis=-1, keepdims=True)
    inv_std = 1.0 / jnp.sqrt(variance + 1e-06)
    normalised = centred * inv_std
    scaled = owned.astype(f32) * gain
    first_mean = jnp.mean(scaled, axis=-1, keepdims=True)
    second_mean = jnp.mean(scaled * normalised, axis=-1, keepdims=True)
    return inv_std * (scaled - first_mean - normalised * second_mean)


def dot(a, b, dims):
    return lax.dot_general(a, b, (dims, ((), ())), preferred_element_type=f32)


def block_power(block):
    largest = jnp.max(jnp.abs(block), axis=(0, 1), keepdims=True)
    scale = jnp.full_like(largest, 2.0**LEAST_POWER)
    power = jnp.full_like(largest, float(LEAST_POWER))
    for step in POWERS:
        fits = largest * (scale * 2.0**step) <= FULL
        scale = jnp.where(fits, scale * 2.0**step, scale)
        power = jnp.where(fits, power + float(step), power)
    return scale, power


def window_start(micro, device, tok_count, slots, offsets_ref):
    start = offsets_ref[micro, device] - device * tok_count
    start = jnp.minimum(jnp.maximum(start, 0), tok_count - slots)
    return start, jnp.minimum(lax.div(start, MAIN), tok_count // MAIN - 3)


def shard_kernel(tok_count, info_ref, counts_ref, offsets_ref, first_ref, second_ref, third_ref, weight_ref, out_ref, cut_ref):
    cols = cut_ref.shape[2]
    for j in range(SIDE):
        cut_ref[j] = weight_ref[:, j * cols : (j + 1) * cols]
    micro, device = info_ref[0], info_ref[1]
    start, base = window_start(micro, device, tok_count, MAIN + REST, offsets_ref)
    delta = start - base * MAIN
    count = counts_ref[micro, device]
    width = first_ref.shape[1]
    chunk = width // REST
    block = jnp.concatenate(
        [first_ref[...].astype(f32), second_ref[...].astype(f32), third_ref[...].astype(f32)], axis=0
    )
    total = block.shape[0]
    block = pltpu.roll(block, lax.rem(total - delta, total), 0)[: MAIN + 2 * REST]
    slot = lax.broadcasted_iota(jnp.int32, block.shape, 0)
    block = jnp.where(slot < count, block, 0.0)
    scale, power = block_power(block)
    block = block * scale
    out_ref[:, :width] = block[:MAIN].astype(bf16)
    pieces = [block[MAIN:, c * chunk : (c + 1) * chunk] for c in range(REST)]
    upper = pieces[0] + pltpu.roll(pieces[1], REST, 0)
    lower = pieces[2] + pltpu.roll(pieces[3], REST, 0)
    out_ref[:, width : width + chunk] = jnp.concatenate([upper, lower], axis=0).astype(bf16)
    out_ref[:, width + chunk :] = jnp.broadcast_to(power, (MAIN, LANES)).astype(bf16)


def image_shard(rows, weight, micro, device, counts, offsets):
    tok_count, width = rows.shape
    own, merge = weight.shape
    info = jnp.stack([micro, device]).astype(jnp.int32)
    out_cols = width + width // REST + LANES

    def at(ahead):
        def index(step, info_ref, counts_ref, offsets_ref):
            return (window_start(info_ref[0], info_ref[1], tok_count, MAIN + REST, offsets_ref)[1] + ahead, 0)

        return pl.BlockSpec((MAIN, width), index)

    return pl.pallas_call(
        functools.partial(shard_kernel, tok_count),
        grid_spec=pltpu.PrefetchScalarGridSpec(
            num_scalar_prefetch=3,
            grid=(1,),
            in_specs=[at(0), at(1), at(2), pl.BlockSpec((own, merge), lambda step, *refs: (0, 0))],
            out_specs=[
                pl.BlockSpec((MAIN, out_cols), lambda step, *refs: (0, 0)),
                pl.BlockSpec((SIDE, own, merge // SIDE), lambda step, *refs: (0, 0, 0)),
            ],
        ),
        out_shape=[
            jax.ShapeDtypeStruct((MAIN, out_cols), bf16),
            jax.ShapeDtypeStruct((SIDE, own, merge // SIDE), bf16),
        ],
        compiler_params=pltpu.CompilerParams(vmem_limit_bytes=VMEM_BYTES),
    )(info, counts, offsets, rows, rows, rows, weight)


def hidden_kernel(source_ref, power_ref, main_ref, tail_ref, slope_ref, out_ref, image_rows):
    main_rows, own = main_ref.shape
    rows = image_rows.shape[0]
    images = main_rows // MAIN
    slots = rows // images
    unscale = jnp.exp2(-power_ref[...])
    row = lax.broadcasted_iota(jnp.int32, (main_rows, own), 0)
    chunk = lax.rem(lax.div(row, REST), REST)
    tail = jnp.zeros((main_rows, own), f32)
    for c in range(REST):
        tail += jnp.where(chunk == c, tail_ref[:, c * own : (c + 1) * own], 0.0)
    tail = (tail * unscale[:, :own]).reshape(images, 2, 2 * REST, own)
    tail = (tail[:, 0] + tail[:, 1]).reshape(main_rows // 2, own)
    tail = tail + pltpu.roll(tail, main_rows // 2 - REST, 0)
    main = main_ref[...] * unscale[:, :own]
    image_rows[...] = jnp.zeros_like(image_rows)
    for i in range(images):
        image_rows[i * slots : i * slots + MAIN, :own] = main[i * MAIN : (i + 1) * MAIN]
        image_rows[i * slots + MAIN : (i + 1) * slots, :own] = tail[i * 2 * REST : i * 2 * REST + REST]
    grad_pre = (image_rows[:, :own] * slope_ref[...]).astype(bf16)
    scale, power = block_power(grad_pre.astype(f32))
    index = lax.broadcasted_iota(jnp.int32, (LANES, rows), 1)
    for part in range(rows // LANES):
        at = slice(part * LANES, (part + 1) * LANES)
        order = jnp.where(index == source_ref[at, :], 1.0, 0.0).astype(bf16)
        image_rows[at, :own] = jnp.dot(order, grad_pre, preferred_element_type=f32) * scale
    out_ref[:, :rows] = image_rows[...].T[:own].astype(bf16)
    out_ref[:, rows:] = jnp.broadcast_to(power, (own, LANES)).astype(bf16)


def hidden_gradient(source, power, main, tail, slope):
    rows, own = slope.shape
    return pl.pallas_call(
        hidden_kernel,
        out_shape=jax.ShapeDtypeStruct((own, rows + LANES), bf16),
        scratch_shapes=[pltpu.VMEM((rows, LANES), f32)],
        compiler_params=pltpu.CompilerParams(vmem_limit_bytes=VMEM_BYTES),
    )(source, power, main, tail, slope)


def pack_kernel(rows_ref, out_ref, packed):
    images = out_ref.shape[0]
    slots = rows_ref.shape[0] // images
    whole = rows_ref.shape[1] // LANES
    rest = rows_ref.shape[1] - whole * LANES
    packed[...] = jnp.zeros_like(packed)
    for i in range(images):
        block = rows_ref[i * slots : (i + 1) * slots, :]
        for c in range(whole):
            packed[i, c * slots : (c + 1) * slots, :] = block[:, c * LANES : (c + 1) * LANES]
        at = slice(whole * slots, whole * slots + slots // 2)
        packed[i, at, :rest] = block[: slots // 2, whole * LANES :]
        packed[i, at, rest:] = block[slots // 2 :, whole * LANES :]
    out_ref[...] = packed[...].astype(bf16)


def packed_rows(rows, images):
    slots = rows.shape[0] // images
    height = -(-slots * rows.shape[1] // LANES // MAIN) * MAIN
    return pl.pallas_call(
        pack_kernel,
        out_shape=jax.ShapeDtypeStruct((images, height, LANES), bf16),
        scratch_shapes=[pltpu.VMEM((images, height, LANES), f32)],
        compiler_params=pltpu.CompilerParams(vmem_limit_bytes=VMEM_BYTES),
    )(rows)


def level_kernel(parts_ref, level_ref, gain_ref, out_ref, sums, owned):
    slots, merge = level_ref.shape
    cols = merge // SIDE
    own = cols // SIDE
    whole = cols // LANES
    rest = cols - whole * LANES
    for y in range(SIDE):
        total = parts_ref[y].astype(f32)
        for z in range(1, SIDE):
            total = total + parts_ref[z * SIDE + y].astype(f32)
        sums[...] = total
        pieces = [sums[c * slots : (c + 1) * slots, :] for c in range(whole)]
        last = sums[whole * slots : whole * slots + slots // 2, :]
        pieces.append(jnp.concatenate([last[:, :rest], last[:, rest:]], axis=0))
        block = jnp.concatenate(pieces, axis=1)
        for z in range(SIDE):
            at = (z * SIDE + y) * own
            owned[:, at : at + own] = block[:, z * own : (z + 1) * own]
    out_ref[...] = norm_backward(level_ref[...], owned[...], gain_ref[...])


def level_rows(parts, level_input, gain):
    slots, merge = level_input.shape
    return pl.pallas_call(
        level_kernel,
        out_shape=jax.ShapeDtypeStruct((slots, merge), f32),
        scratch_shapes=[pltpu.VMEM(parts.shape[1:], f32), pltpu.VMEM((slots, merge), f32)],
        compiler_params=pltpu.CompilerParams(vmem_limit_bytes=VMEM_BYTES),
    )(parts, level_input, gain)


def body(llm_grad, counts, offsets, owner, w_up, w_down, pre_act, fc1_input, level_input, ln_gain):
    z_index = lax.axis_index("z")
    y_index = lax.axis_index("y")
    device_index = z_index * SIDE + y_index
    section_index = lax.axis_index("section")
    micro_index = section_index // LEVELS
    level_index = section_index % LEVELS
    tok_count, width = llm_grad.shape[1:]
    slots = level_input.shape[1]
    images = counts.shape[1]
    rows = images * slots
    own = w_up.shape[1]
    merge = w_up.shape[2]
    chunk = width // REST
    main_rows = images * MAIN

    shard, weight = image_shard(llm_grad[0], w_up[0], micro_index, device_index, counts, offsets)
    gathered = lax.all_gather(shard.astype(f16), ("z", "y"), axis=0, tiled=True)
    feed = jnp.broadcast_to(fc1_input[0].T[None], (SIDE, own, rows))

    owner_row = lax.dynamic_index_in_dim(owner, micro_index, 0, keepdims=False)
    number = jnp.arange(images, dtype=jnp.int32)
    slot = jnp.arange(slots, dtype=jnp.int32)[None, :]
    inverse = jnp.sum(jnp.where(owner_row[None, :] == number[:, None], number[None, :], 0), axis=1)
    source = (inverse[:, None] * slots + slot).reshape(rows, 1).astype(jnp.int32)
    place = (owner_row[:, None] * slots + slot).reshape(rows)

    pre = pre_act[0].astype(f32)
    slope = gelu_parts(pre)[1]
    down = w_down[0]
    tail_weight = jnp.concatenate([down[:, c * chunk : (c + 1) * chunk] for c in range(REST)], axis=0)
    gathered, feed, slope, source, tail_weight, weight = lax.optimization_barrier(
        (gathered, feed, slope, source, tail_weight, weight)
    )

    power = gathered[:, width + chunk :].astype(f32)
    hidden_main = dot(gathered[:, :width].astype(bf16), down, ((1,), (1,)))
    hidden_tail = dot(gathered[:, width : width + chunk].astype(bf16), tail_weight, ((1,), (1,)))
    grad_pre = hidden_gradient(source, power, hidden_main, hidden_tail, slope)
    panel = lax.all_gather(grad_pre.astype(f16), "y", axis=0, tiled=True)
    weight = lax.all_to_all(weight, "z", split_axis=0, concat_axis=0).reshape(SIDE * own, SIDE * own)
    feed = lax.all_to_all(feed, "z", split_axis=0, concat_axis=0).reshape(SIDE * own, rows)
    panel, weight = lax.optimization_barrier((panel, weight))
    panel = (panel[:, :rows].astype(f32) * jnp.exp2(-panel[:, rows : rows + 1].astype(f32))).astype(bf16)

    parts = packed_rows(dot(panel, weight, ((0,), (1,))), images)
    parts = lax.all_to_all(parts, ("z", "y"), split_axis=0, concat_axis=0)

    to_owner = (place[:, None] == jnp.arange(rows, dtype=jnp.int32)[None, :]).astype(bf16)
    feed = dot(feed, to_owner, ((1,), (0,))).astype(bf16)
    grad_up = dot(feed, panel, ((1,), (1,))).astype(bf16).reshape(SIDE, own, SIDE * own)
    grad_up = lax.all_to_all(grad_up, "z", split_axis=0, concat_axis=0)
    grad_up = grad_up.transpose(1, 0, 2).reshape(own, merge)

    unscale = jnp.exp2(-power[:, :1])
    activated = gelu_parts(pre)[0].astype(bf16).reshape(images, slots, own)
    row_chunk = (jnp.arange(main_rows, dtype=jnp.int32) // REST) % REST
    same_chunk = row_chunk[:, None] == jnp.arange(REST * own, dtype=jnp.int32)[None, :] // own
    act_main = (activated[:, :MAIN].reshape(main_rows, own).astype(f32) * unscale).astype(bf16)
    act_tail = jnp.broadcast_to(activated[:, None, MAIN:, None, :], (images, REST, REST, REST, own))
    act_tail = act_tail.reshape(main_rows, REST * own).astype(f32) * unscale
    act_tail = jnp.where(same_chunk, act_tail, 0.0).astype(bf16)
    grad_down = dot(act_main, gathered[:, :width].astype(bf16), ((0,), (0,)))
    grad_down_tail = dot(act_tail, gathered[:, width : width + chunk].astype(bf16), ((0,), (0,)))
    grad_down_tail = grad_down_tail.reshape(REST, own, chunk).transpose(1, 0, 2).reshape(own, width)
    grad_down = (grad_down + grad_down_tail).astype(bf16)
    parts, grad_up, grad_down = lax.optimization_barrier((parts, grad_up, grad_down))
    level_part = level_rows(parts, level_input[0], ln_gain)

    count = lax.axis_size("section")
    other = lax.ppermute(level_part, "section", [(source, source ^ 1) for source in range(count)])
    pair_sum = level_part + other
    below = [(source, source - 2) for source in range(count) if source % LEVELS >= 2]
    above = lax.ppermute(pair_sum.astype(bf16), "section", below).astype(f32)
    summed = jnp.where(level_index % 2 == 0, pair_sum, level_part)
    summed = summed + jnp.where(level_index < 2, above, 0.0)
    return (summed.astype(bf16)[None], grad_up[None], grad_down[None])


def solution(mesh):
    sections = mesh.devices.shape[0]
    cube = Mesh(mesh.devices.reshape(sections, SIDE, SIDE), ("section", "z", "y"))
    rows = P("section", ("z", "y"), None)
    cols = P("section", None, ("z", "y"))
    return jax.shard_map(
        body,
        mesh=cube,
        in_specs=(rows, P(), P(), P(), rows, rows, cols, cols, rows, P("section", None)),
        out_specs=(rows, rows, rows),
        check_vma=False,
    )
```

```python
import functools

import jax
import jax.numpy as jnp
from jax import lax
from jax.experimental import pallas as pl
from jax.experimental.pallas import tpu as pltpu
from jax.sharding import Mesh, PartitionSpec as P

inv_sqrt_two = 0.7071067811865476
inv_sqrt_two_pi = 0.3989422804014327
f32 = jnp.float32
bf16 = jnp.bfloat16
f16 = jnp.float16

SIDE = 8
LEVELS = 4
MAIN = 16
REST = 4
LANES = 128
VMEM_BYTES = 20 * 1024 * 1024
FULL = 32768.0
LEAST_POWER = -113
POWERS = (86, 64, 32, 16, 8, 4, 2, 1)


def gelu_parts(pre_float):
    cdf_part = 0.5 * (1.0 + jax.scipy.special.erf(pre_float * inv_sqrt_two))
    activated = pre_float * cdf_part
    slope = cdf_part + pre_float * jnp.exp(-0.5 * pre_float * pre_float) * inv_sqrt_two_pi
    return (activated, slope)


def norm_backward(level_rows, owned, gain):
    x_float = level_rows.astype(f32)
    row_mean = jnp.mean(x_float, axis=-1, keepdims=True)
    centred = x_float - row_mean
    variance = jnp.mean(centred * centred, axis=-1, keepdims=True)
    inv_std = 1.0 / jnp.sqrt(variance + 1e-06)
    normalised = centred * inv_std
    scaled = owned.astype(f32) * gain
    first_mean = jnp.mean(scaled, axis=-1, keepdims=True)
    second_mean = jnp.mean(scaled * normalised, axis=-1, keepdims=True)
    return inv_std * (scaled - first_mean - normalised * second_mean)


def dot(a, b, dims):
    return lax.dot_general(a, b, (dims, ((), ())), preferred_element_type=f32)


def block_power(block):
    largest = jnp.max(jnp.abs(block), axis=(0, 1), keepdims=True)
    scale = jnp.full_like(largest, 2.0**LEAST_POWER)
    power = jnp.full_like(largest, float(LEAST_POWER))
    for step in POWERS:
        fits = largest * (scale * 2.0**step) <= FULL
        scale = jnp.where(fits, scale * 2.0**step, scale)
        power = jnp.where(fits, power + float(step), power)
    return scale, power


def window_start(micro, device, tok_count, slots, offsets_ref):
    start = offsets_ref[micro, device] - device * tok_count
    start = jnp.minimum(jnp.maximum(start, 0), tok_count - slots)
    return start, jnp.minimum(lax.div(start, MAIN), tok_count // MAIN - 3)


def shard_kernel(tok_count, info_ref, counts_ref, offsets_ref, first_ref, second_ref, third_ref, weight_ref, down_ref, out_ref, cut_ref, down_cut_ref):
    for source_ref, blocks_ref in ((weight_ref, cut_ref), (down_ref, down_cut_ref)):
        cols = blocks_ref.shape[2]
        for j in range(blocks_ref.shape[0]):
            blocks_ref[j] = source_ref[:, j * cols : (j + 1) * cols]
    micro, device = info_ref[0], info_ref[1]
    start, base = window_start(micro, device, tok_count, MAIN + REST, offsets_ref)
    delta = start - base * MAIN
    count = counts_ref[micro, device]
    width = first_ref.shape[1]
    chunk = width // REST
    block = jnp.concatenate(
        [first_ref[...].astype(f32), second_ref[...].astype(f32), third_ref[...].astype(f32)], axis=0
    )
    total = block.shape[0]
    block = pltpu.roll(block, lax.rem(total - delta, total), 0)[: MAIN + 2 * REST]
    slot = lax.broadcasted_iota(jnp.int32, block.shape, 0)
    block = jnp.where(slot < count, block, 0.0)
    scale, power = block_power(block)
    block = block * scale
    out_ref[:, :width] = block[:MAIN].astype(bf16)
    pieces = [block[MAIN:, c * chunk : (c + 1) * chunk] for c in range(REST)]
    upper = pieces[0] + pltpu.roll(pieces[1], REST, 0)
    lower = pieces[2] + pltpu.roll(pieces[3], REST, 0)
    out_ref[:, width : width + chunk] = jnp.concatenate([upper, lower], axis=0).astype(bf16)
    out_ref[:, width + chunk :] = jnp.broadcast_to(power, (MAIN, LANES)).astype(bf16)


def image_shard(rows, weight, down, micro, device, counts, offsets):
    tok_count, width = rows.shape
    own, merge = weight.shape
    info = jnp.stack([micro, device]).astype(jnp.int32)
    out_cols = width + width // REST + LANES

    def at(ahead):
        def index(step, info_ref, counts_ref, offsets_ref):
            return (window_start(info_ref[0], info_ref[1], tok_count, MAIN + REST, offsets_ref)[1] + ahead, 0)

        return pl.BlockSpec((MAIN, width), index)

    return pl.pallas_call(
        functools.partial(shard_kernel, tok_count),
        grid_spec=pltpu.PrefetchScalarGridSpec(
            num_scalar_prefetch=3,
            grid=(1,),
            in_specs=[
                at(0),
                at(1),
                at(2),
                pl.BlockSpec((own, merge), lambda step, *refs: (0, 0)),
                pl.BlockSpec((own, width), lambda step, *refs: (0, 0)),
            ],
            out_specs=[
                pl.BlockSpec((MAIN, out_cols), lambda step, *refs: (0, 0)),
                pl.BlockSpec((SIDE, own, merge // SIDE), lambda step, *refs: (0, 0, 0)),
                pl.BlockSpec((REST, own, width // REST), lambda step, *refs: (0, 0, 0)),
            ],
        ),
        out_shape=[
            jax.ShapeDtypeStruct((MAIN, out_cols), bf16),
            jax.ShapeDtypeStruct((SIDE, own, merge // SIDE), bf16),
            jax.ShapeDtypeStruct((REST, own, width // REST), bf16),
        ],
        compiler_params=pltpu.CompilerParams(vmem_limit_bytes=3 * VMEM_BYTES),
    )(info, counts, offsets, rows, rows, rows, weight, down)


def hidden_kernel(source_ref, power_ref, main_ref, tail_ref, pre_ref, out_ref, image_rows):
    main_rows, own = main_ref.shape
    rows = image_rows.shape[0]
    images = main_rows // MAIN
    slots = rows // images
    unscale = jnp.exp2(-power_ref[...])[:, :own]
    row = lax.broadcasted_iota(jnp.int32, (main_rows, own), 0)
    chunk = lax.rem(lax.div(row, REST), REST)
    tail = jnp.zeros((main_rows, own), f32)
    for c in range(REST):
        tail += jnp.where(chunk == c, tail_ref[:, c * own : (c + 1) * own], 0.0)
    tail = (tail * unscale).reshape(images, 2, 2 * REST, own)
    tail = (tail[:, 0] + tail[:, 1]).reshape(main_rows // 2, own)
    tail = tail + pltpu.roll(tail, main_rows // 2 - REST, 0)
    main = main_ref[...] * unscale
    image_rows[...] = jnp.zeros_like(image_rows)
    for i in range(images):
        image_rows[i * slots : i * slots + MAIN, :own] = main[i * MAIN : (i + 1) * MAIN]
        image_rows[i * slots + MAIN : (i + 1) * slots, :own] = tail[i * 2 * REST : i * 2 * REST + REST]
    slope = gelu_parts(pre_ref[...].astype(f32))[1]
    grad_pre = (image_rows[...].T[:own] * slope).astype(bf16)
    scale, power = block_power(grad_pre.astype(f32))
    index = lax.broadcasted_iota(jnp.int32, (rows, 2 * LANES), 0)
    for part in range(rows // (2 * LANES)):
        at = slice(part * 2 * LANES, (part + 1) * 2 * LANES)
        order = jnp.where(index == source_ref[:, at], 1.0, 0.0).astype(bf16)
        out_ref[:, at] = (jnp.dot(grad_pre, order, preferred_element_type=f32) * scale).astype(bf16)
    out_ref[:, rows:] = jnp.broadcast_to(power, (own, LANES)).astype(bf16)


def hidden_gradient(source, power, main, tail, pre):
    own, rows = pre.shape
    return pl.pallas_call(
        hidden_kernel,
        out_shape=jax.ShapeDtypeStruct((own, rows + LANES), bf16),
        scratch_shapes=[pltpu.VMEM((rows, LANES), f32)],
        compiler_params=pltpu.CompilerParams(vmem_limit_bytes=VMEM_BYTES),
    )(source, power, main, tail, pre)


def activation_kernel(power_ref, pre_ref, main_ref, tail_ref, image_rows, spread):
    main_rows, own = main_ref.shape
    rows = image_rows.shape[0]
    images = main_rows // MAIN
    slots = rows // images
    unscale = jnp.exp2(-power_ref[...])
    activated = gelu_parts(pre_ref[...].astype(f32))[0].astype(bf16).astype(f32)
    pad = jnp.zeros((LANES - own, rows), f32)
    image_rows[...] = jnp.concatenate([activated, pad], axis=0).T
    for i in range(images):
        spread[i * MAIN : (i + 1) * MAIN, :] = image_rows[i * slots : i * slots + MAIN, :]
    main_ref[...] = (spread[...] * unscale)[:, :own].astype(bf16)
    for i in range(images):
        for c in range(REST):
            at = i * MAIN + c * REST
            spread[at : at + REST, :] = image_rows[i * slots + MAIN : (i + 1) * slots, :]
    tail = (spread[...] * unscale)[:, :own]
    row = lax.broadcasted_iota(jnp.int32, (main_rows, own), 0)
    chunk = lax.rem(lax.div(row, REST), REST)
    for c in range(REST):
        tail_ref[:, c * own : (c + 1) * own] = jnp.where(chunk == c, tail, 0.0).astype(bf16)


def activations(power, pre):
    own, rows = pre.shape
    main_rows = power.shape[0]
    return pl.pallas_call(
        activation_kernel,
        out_shape=[
            jax.ShapeDtypeStruct((main_rows, own), bf16),
            jax.ShapeDtypeStruct((main_rows, REST * own), bf16),
        ],
        scratch_shapes=[pltpu.VMEM((rows, LANES), f32), pltpu.VMEM((main_rows, LANES), f32)],
        compiler_params=pltpu.CompilerParams(vmem_limit_bytes=VMEM_BYTES),
    )(power, pre)


def pack_kernel(rows_ref, out_ref, packed):
    images = out_ref.shape[0]
    slots = rows_ref.shape[0] // images
    whole = rows_ref.shape[1] // LANES
    rest = rows_ref.shape[1] - whole * LANES
    packed[...] = jnp.zeros_like(packed)
    for i in range(images):
        block = rows_ref[i * slots : (i + 1) * slots, :]
        for c in range(whole):
            packed[i, c * slots : (c + 1) * slots, :] = block[:, c * LANES : (c + 1) * LANES]
        at = slice(whole * slots, whole * slots + slots // 2)
        packed[i, at, :rest] = block[: slots // 2, whole * LANES :]
        packed[i, at, rest:] = block[slots // 2 :, whole * LANES :]
    out_ref[...] = packed[...].astype(bf16)


def packed_rows(rows, images):
    slots = rows.shape[0] // images
    height = -(-slots * rows.shape[1] // LANES // MAIN) * MAIN
    return pl.pallas_call(
        pack_kernel,
        out_shape=jax.ShapeDtypeStruct((images, height, LANES), bf16),
        scratch_shapes=[pltpu.VMEM((images, height, LANES), f32)],
        compiler_params=pltpu.CompilerParams(vmem_limit_bytes=VMEM_BYTES),
    )(rows)


def level_kernel(parts_ref, level_ref, gain_ref, out_ref, sums, owned):
    slots, merge = level_ref.shape
    cols = merge // SIDE
    own = cols // SIDE
    whole = cols // LANES
    rest = cols - whole * LANES
    for y in range(SIDE):
        total = parts_ref[y].astype(f32)
        for z in range(1, SIDE):
            total = total + parts_ref[z * SIDE + y].astype(f32)
        sums[...] = total
        pieces = [sums[c * slots : (c + 1) * slots, :] for c in range(whole)]
        last = sums[whole * slots : whole * slots + slots // 2, :]
        pieces.append(jnp.concatenate([last[:, :rest], last[:, rest:]], axis=0))
        block = jnp.concatenate(pieces, axis=1)
        for z in range(SIDE):
            at = (z * SIDE + y) * own
            owned[:, at : at + own] = block[:, z * own : (z + 1) * own]
    out_ref[...] = norm_backward(level_ref[...], owned[...], gain_ref[...])


def level_rows(parts, level_input, gain):
    slots, merge = level_input.shape
    return pl.pallas_call(
        level_kernel,
        out_shape=jax.ShapeDtypeStruct((slots, merge), f32),
        scratch_shapes=[pltpu.VMEM(parts.shape[1:], f32), pltpu.VMEM((slots, merge), f32)],
        compiler_params=pltpu.CompilerParams(vmem_limit_bytes=VMEM_BYTES),
    )(parts, level_input, gain)


def body(llm_grad, counts, offsets, owner, w_up, w_down, pre_act, fc1_input, level_input, ln_gain):
    z_index = lax.axis_index("z")
    y_index = lax.axis_index("y")
    device_index = z_index * SIDE + y_index
    section_index = lax.axis_index("section")
    micro_index = section_index // LEVELS
    level_index = section_index % LEVELS
    tok_count, width = llm_grad.shape[1:]
    slots = level_input.shape[1]
    images = counts.shape[1]
    rows = images * slots
    own = w_up.shape[1]
    merge = w_up.shape[2]
    chunk = width // REST

    down = w_down[0]
    shard, weight, down_tail = image_shard(
        llm_grad[0], w_up[0], down, micro_index, device_index, counts, offsets
    )
    gathered = lax.all_gather(shard.astype(f16), ("z", "y"), axis=0, tiled=True)
    feed = fc1_input[0].T

    owner_row = lax.dynamic_index_in_dim(owner, micro_index, 0, keepdims=False)
    number = jnp.arange(images, dtype=jnp.int32)
    slot = jnp.arange(slots, dtype=jnp.int32)[None, :]
    inverse = jnp.sum(jnp.where(owner_row[None, :] == number[:, None], number[None, :], 0), axis=1)
    source = (inverse[:, None] * slots + slot).reshape(1, rows).astype(jnp.int32)
    place = (owner_row[:, None] * slots + slot).reshape(rows)
    pre = pre_act[0].T
    gathered, weight, source, down_tail = lax.optimization_barrier((gathered, weight, source, down_tail))

    weight = lax.all_to_all(weight, "z", split_axis=0, concat_axis=0).reshape(SIDE * own, SIDE * own)
    power = gathered[:, width + chunk :].astype(f32)
    hidden_main = dot(gathered[:, :width].astype(bf16), down, ((1,), (1,)))
    hidden_tail = dot(
        gathered[:, width : width + chunk].astype(bf16), down_tail.reshape(REST * own, chunk), ((1,), (1,))
    )
    grad_pre = hidden_gradient(source, power, hidden_main, hidden_tail, pre)
    feed, grad_pre = lax.optimization_barrier((feed, grad_pre))
    feed = jnp.broadcast_to(feed[None], (SIDE, own, rows))
    weight, feed, grad_pre = lax.optimization_barrier((weight, feed, grad_pre))
    feed = lax.all_to_all(feed, "z", split_axis=0, concat_axis=0).reshape(SIDE * own, rows)
    panel = lax.all_gather(grad_pre.astype(f16), "y", axis=0, tiled=True)
    panel, feed = lax.optimization_barrier((panel, feed))

    def scaled_back(block):
        return (block[:, :rows].astype(f32) * jnp.exp2(-block[:, rows : rows + 1].astype(f32))).astype(bf16)

    parts = packed_rows(dot(scaled_back(panel), weight, ((0,), (1,))), images)
    parts, panel, feed, place, gathered, power = lax.optimization_barrier(
        (parts, panel, feed, place, gathered, power)
    )
    parts = lax.all_to_all(parts, ("z", "y"), split_axis=0, concat_axis=0)

    to_owner = (place[:, None] == jnp.arange(rows, dtype=jnp.int32)[None, :]).astype(bf16)
    feed = dot(feed, to_owner, ((1,), (0,))).astype(bf16)
    grad_up = dot(feed, scaled_back(panel), ((1,), (1,))).astype(bf16).reshape(SIDE, own, SIDE * own)
    act_main, act_tail = activations(power, pre)
    grad_down = dot(act_main, gathered[:, :width].astype(bf16), ((0,), (0,)))
    grad_down_tail = dot(act_tail, gathered[:, width : width + chunk].astype(bf16), ((0,), (0,)))
    grad_down_tail = grad_down_tail.reshape(REST, own, chunk).transpose(1, 0, 2).reshape(own, width)
    grad_down = (grad_down + grad_down_tail).astype(bf16)
    parts, grad_up, grad_down = lax.optimization_barrier((parts, grad_up, grad_down))

    grad_up = lax.all_to_all(grad_up, "z", split_axis=0, concat_axis=0)
    grad_up = grad_up.transpose(1, 0, 2).reshape(own, merge)
    level_part = level_rows(parts, level_input[0], ln_gain)

    count = lax.axis_size("section")
    other = lax.ppermute(level_part, "section", [(source, source ^ 1) for source in range(count)])
    pair_sum = level_part + other
    below = [(source, source - 2) for source in range(count) if source % LEVELS >= 2]
    above = lax.ppermute(pair_sum.astype(bf16), "section", below)
    above, grad_up = lax.optimization_barrier((above, grad_up))
    above = above.astype(f32)
    summed = jnp.where(level_index % 2 == 0, pair_sum, level_part)
    summed = summed + jnp.where(level_index < 2, above, 0.0)
    return (summed.astype(bf16)[None], grad_up[None], grad_down[None])


def solution(mesh):
    sections = mesh.devices.shape[0]
    cube = Mesh(mesh.devices.reshape(sections, SIDE, SIDE), ("section", "z", "y"))
    rows = P("section", ("z", "y"), None)
    cols = P("section", None, ("z", "y"))
    return jax.shard_map(
        body,
        mesh=cube,
        in_specs=(rows, P(), P(), P(), rows, rows, cols, cols, rows, P("section", None)),
        out_specs=(rows, rows, rows),
        check_vma=False,
    )
```

```python
import functools

import jax
import jax.numpy as jnp
from jax import lax
from jax.experimental import pallas as pl
from jax.experimental.pallas import tpu as pltpu
from jax.sharding import Mesh, PartitionSpec as P

inv_sqrt_two = 0.7071067811865476
inv_sqrt_two_pi = 0.3989422804014327
f32 = jnp.float32
bf16 = jnp.bfloat16
f16 = jnp.float16

SIDE = 8
LEVELS = 4
MAIN = 16
REST = 4
LANES = 128
VMEM_BYTES = 20 * 1024 * 1024
FULL = 32768.0
LEAST_POWER = -113
POWERS = (86, 64, 32, 16, 8, 4, 2, 1)


def gelu_parts(pre_float):
    cdf_part = 0.5 * (1.0 + jax.scipy.special.erf(pre_float * inv_sqrt_two))
    activated = pre_float * cdf_part
    slope = cdf_part + pre_float * jnp.exp(-0.5 * pre_float * pre_float) * inv_sqrt_two_pi
    return (activated, slope)


def norm_backward(level_rows, owned, gain):
    x_float = level_rows.astype(f32)
    row_mean = jnp.mean(x_float, axis=-1, keepdims=True)
    centred = x_float - row_mean
    variance = jnp.mean(centred * centred, axis=-1, keepdims=True)
    inv_std = 1.0 / jnp.sqrt(variance + 1e-06)
    normalised = centred * inv_std
    scaled = owned.astype(f32) * gain
    first_mean = jnp.mean(scaled, axis=-1, keepdims=True)
    second_mean = jnp.mean(scaled * normalised, axis=-1, keepdims=True)
    return inv_std * (scaled - first_mean - normalised * second_mean)


def dot(a, b, dims):
    return lax.dot_general(a, b, (dims, ((), ())), preferred_element_type=f32)


def block_power(block):
    largest = jnp.max(jnp.abs(block), axis=(0, 1), keepdims=True)
    scale = jnp.full_like(largest, 2.0**LEAST_POWER)
    power = jnp.full_like(largest, float(LEAST_POWER))
    for step in POWERS:
        fits = largest * (scale * 2.0**step) <= FULL
        scale = jnp.where(fits, scale * 2.0**step, scale)
        power = jnp.where(fits, power + float(step), power)
    return scale, power


def window_start(micro, device, tok_count, slots, offsets_ref):
    start = offsets_ref[micro, device] - device * tok_count
    start = jnp.minimum(jnp.maximum(start, 0), tok_count - slots)
    return start, jnp.minimum(lax.div(start, MAIN), tok_count // MAIN - 3)


def shard_kernel(tok_count, info_ref, counts_ref, offsets_ref, first_ref, second_ref, third_ref, weight_ref, down_ref, out_ref, cut_ref, down_cut_ref):
    cols = cut_ref.shape[2]
    own = cols // SIDE

    @pl.when(info_ref[2] == 0)
    def _():
        for j in range(SIDE):
            cut_ref[j] = weight_ref[:, j * cols : (j + 1) * cols]

    @pl.when(info_ref[2] == 1)
    def _():
        for j in range(SIDE):
            for k in range(SIDE):
                at = (k * SIDE + j) * own
                cut_ref[j, :, k * own : (k + 1) * own] = weight_ref[:, at : at + own]

    cols = down_cut_ref.shape[2]
    for j in range(REST):
        down_cut_ref[j] = down_ref[:, j * cols : (j + 1) * cols]
    micro, device = info_ref[0], info_ref[1]
    start, base = window_start(micro, device, tok_count, MAIN + REST, offsets_ref)
    delta = start - base * MAIN
    count = counts_ref[micro, device]
    width = first_ref.shape[1]
    chunk = width // REST
    block = jnp.concatenate(
        [first_ref[...].astype(f32), second_ref[...].astype(f32), third_ref[...].astype(f32)], axis=0
    )
    total = block.shape[0]
    block = pltpu.roll(block, lax.rem(total - delta, total), 0)[: MAIN + 2 * REST]
    slot = lax.broadcasted_iota(jnp.int32, block.shape, 0)
    block = jnp.where(slot < count, block, 0.0)
    scale, power = block_power(block)
    block = block * scale
    out_ref[:, :width] = block[:MAIN].astype(bf16)
    pieces = [block[MAIN:, c * chunk : (c + 1) * chunk] for c in range(REST)]
    upper = pieces[0] + pltpu.roll(pieces[1], REST, 0)
    lower = pieces[2] + pltpu.roll(pieces[3], REST, 0)
    out_ref[:, width : width + chunk] = jnp.concatenate([upper, lower], axis=0).astype(bf16)
    out_ref[:, width + chunk :] = jnp.broadcast_to(power, (MAIN, LANES)).astype(bf16)


def image_shard(rows, weight, down, micro, device, swapped, counts, offsets):
    tok_count, width = rows.shape
    own, merge = weight.shape
    info = jnp.stack([micro, device, swapped]).astype(jnp.int32)
    out_cols = width + width // REST + LANES

    def at(ahead):
        def index(step, info_ref, counts_ref, offsets_ref):
            return (window_start(info_ref[0], info_ref[1], tok_count, MAIN + REST, offsets_ref)[1] + ahead, 0)

        return pl.BlockSpec((MAIN, width), index)

    return pl.pallas_call(
        functools.partial(shard_kernel, tok_count),
        grid_spec=pltpu.PrefetchScalarGridSpec(
            num_scalar_prefetch=3,
            grid=(1,),
            in_specs=[
                at(0),
                at(1),
                at(2),
                pl.BlockSpec((own, merge), lambda step, *refs: (0, 0)),
                pl.BlockSpec((own, width), lambda step, *refs: (0, 0)),
            ],
            out_specs=[
                pl.BlockSpec((MAIN, out_cols), lambda step, *refs: (0, 0)),
                pl.BlockSpec((SIDE, own, merge // SIDE), lambda step, *refs: (0, 0, 0)),
                pl.BlockSpec((REST, own, width // REST), lambda step, *refs: (0, 0, 0)),
            ],
        ),
        out_shape=[
            jax.ShapeDtypeStruct((MAIN, out_cols), bf16),
            jax.ShapeDtypeStruct((SIDE, own, merge // SIDE), bf16),
            jax.ShapeDtypeStruct((REST, own, width // REST), bf16),
        ],
        compiler_params=pltpu.CompilerParams(vmem_limit_bytes=3 * VMEM_BYTES),
    )(info, counts, offsets, rows, rows, rows, weight, down)


def hidden_kernel(source_ref, power_ref, main_ref, tail_ref, pre_ref, feed_ref, out_ref, copies_ref, image_rows):
    for j in range(SIDE):
        copies_ref[j] = feed_ref[...]
    main_rows, own = main_ref.shape
    rows = image_rows.shape[0]
    images = main_rows // MAIN
    slots = rows // images
    unscale = jnp.exp2(-power_ref[...])[:, :own]
    row = lax.broadcasted_iota(jnp.int32, (main_rows, own), 0)
    chunk = lax.rem(lax.div(row, REST), REST)
    tail = jnp.zeros((main_rows, own), f32)
    for c in range(REST):
        tail += jnp.where(chunk == c, tail_ref[:, c * own : (c + 1) * own], 0.0)
    tail = (tail * unscale).reshape(images, 2, 2 * REST, own)
    tail = (tail[:, 0] + tail[:, 1]).reshape(main_rows // 2, own)
    tail = tail + pltpu.roll(tail, main_rows // 2 - REST, 0)
    main = main_ref[...] * unscale
    image_rows[...] = jnp.zeros_like(image_rows)
    for i in range(images):
        image_rows[i * slots : i * slots + MAIN, :own] = main[i * MAIN : (i + 1) * MAIN]
        image_rows[i * slots + MAIN : (i + 1) * slots, :own] = tail[i * 2 * REST : i * 2 * REST + REST]
    slope = gelu_parts(pre_ref[...].astype(f32))[1]
    grad_pre = (image_rows[...].T[:own] * slope).astype(bf16)
    scale, power = block_power(grad_pre.astype(f32))
    index = lax.broadcasted_iota(jnp.int32, (rows, 2 * LANES), 0)
    for part in range(rows // (2 * LANES)):
        at = slice(part * 2 * LANES, (part + 1) * 2 * LANES)
        order = jnp.where(index == source_ref[:, at], 1.0, 0.0).astype(bf16)
        out_ref[:, at] = (jnp.dot(grad_pre, order, preferred_element_type=f32) * scale).astype(bf16)
    out_ref[:, rows:] = jnp.broadcast_to(power, (own, LANES)).astype(bf16)


def hidden_gradient(source, power, main, tail, pre, feed):
    own, rows = pre.shape
    return pl.pallas_call(
        hidden_kernel,
        out_shape=[
            jax.ShapeDtypeStruct((own, rows + LANES), bf16),
            jax.ShapeDtypeStruct((SIDE, own, rows), bf16),
        ],
        scratch_shapes=[pltpu.VMEM((rows, LANES), f32)],
        compiler_params=pltpu.CompilerParams(vmem_limit_bytes=VMEM_BYTES),
    )(source, power, main, tail, pre, feed)


def activation_kernel(power_ref, pre_ref, main_ref, tail_ref, image_rows, spread):
    main_rows, own = main_ref.shape
    rows = image_rows.shape[0]
    images = main_rows // MAIN
    slots = rows // images
    unscale = jnp.exp2(-power_ref[...])
    activated = gelu_parts(pre_ref[...].astype(f32))[0].astype(bf16).astype(f32)
    pad = jnp.zeros((LANES - own, rows), f32)
    image_rows[...] = jnp.concatenate([activated, pad], axis=0).T
    for i in range(images):
        spread[i * MAIN : (i + 1) * MAIN, :] = image_rows[i * slots : i * slots + MAIN, :]
    main_ref[...] = (spread[...] * unscale)[:, :own].astype(bf16)
    for i in range(images):
        for c in range(REST):
            at = i * MAIN + c * REST
            spread[at : at + REST, :] = image_rows[i * slots + MAIN : (i + 1) * slots, :]
    tail = (spread[...] * unscale)[:, :own]
    row = lax.broadcasted_iota(jnp.int32, (main_rows, own), 0)
    chunk = lax.rem(lax.div(row, REST), REST)
    for c in range(REST):
        tail_ref[:, c * own : (c + 1) * own] = jnp.where(chunk == c, tail, 0.0).astype(bf16)


def activations(power, pre):
    own, rows = pre.shape
    main_rows = power.shape[0]
    return pl.pallas_call(
        activation_kernel,
        out_shape=[
            jax.ShapeDtypeStruct((main_rows, own), bf16),
            jax.ShapeDtypeStruct((main_rows, REST * own), bf16),
        ],
        scratch_shapes=[pltpu.VMEM((rows, LANES), f32), pltpu.VMEM((main_rows, LANES), f32)],
        compiler_params=pltpu.CompilerParams(vmem_limit_bytes=VMEM_BYTES),
    )(power, pre)


def pack_kernel(rows_ref, out_ref, packed):
    images = out_ref.shape[0]
    slots = rows_ref.shape[0] // images
    whole = rows_ref.shape[1] // LANES
    rest = rows_ref.shape[1] - whole * LANES
    packed[...] = jnp.zeros_like(packed)
    for i in range(images):
        block = rows_ref[i * slots : (i + 1) * slots, :]
        for c in range(whole):
            packed[i, c * slots : (c + 1) * slots, :] = block[:, c * LANES : (c + 1) * LANES]
        at = slice(whole * slots, whole * slots + slots // 2)
        packed[i, at, :rest] = block[: slots // 2, whole * LANES :]
        packed[i, at, rest:] = block[slots // 2 :, whole * LANES :]
    out_ref[...] = packed[...].astype(bf16)


def packed_rows(rows, images):
    slots = rows.shape[0] // images
    height = -(-slots * rows.shape[1] // LANES // MAIN) * MAIN
    return pl.pallas_call(
        pack_kernel,
        out_shape=jax.ShapeDtypeStruct((images, height, LANES), bf16),
        scratch_shapes=[pltpu.VMEM((images, height, LANES), f32)],
        compiler_params=pltpu.CompilerParams(vmem_limit_bytes=VMEM_BYTES),
    )(rows)


def level_kernel(swapped_ref, parts_ref, level_ref, gain_ref, out_ref, sums, owned):
    slots, merge = level_ref.shape
    cols = merge // SIDE
    own = cols // SIDE
    whole = cols // LANES
    rest = cols - whole * LANES

    def summed(sources):
        total = parts_ref[sources[0]].astype(f32)
        for source in sources[1:]:
            total = total + parts_ref[source].astype(f32)
        sums[...] = total
        pieces = [sums[c * slots : (c + 1) * slots, :] for c in range(whole)]
        last = sums[whole * slots : whole * slots + slots // 2, :]
        pieces.append(jnp.concatenate([last[:, :rest], last[:, rest:]], axis=0))
        return jnp.concatenate(pieces, axis=1)

    @pl.when(swapped_ref[0] == 0)
    def _():
        for y in range(SIDE):
            block = summed([z * SIDE + y for z in range(SIDE)])
            for z in range(SIDE):
                at = (z * SIDE + y) * own
                owned[:, at : at + own] = block[:, z * own : (z + 1) * own]

    @pl.when(swapped_ref[0] == 1)
    def _():
        for z in range(SIDE):
            owned[:, z * cols : (z + 1) * cols] = summed([z * SIDE + y for y in range(SIDE)])

    out_ref[...] = norm_backward(level_ref[...], owned[...], gain_ref[...])


def level_rows(swapped, parts, level_input, gain):
    slots, merge = level_input.shape
    vmem = pl.BlockSpec(memory_space=pltpu.VMEM)
    return pl.pallas_call(
        level_kernel,
        in_specs=[pl.BlockSpec(memory_space=pltpu.SMEM), vmem, vmem, vmem],
        out_shape=jax.ShapeDtypeStruct((slots, merge), f32),
        scratch_shapes=[pltpu.VMEM(parts.shape[1:], f32), pltpu.VMEM((slots, merge), f32)],
        compiler_params=pltpu.CompilerParams(vmem_limit_bytes=VMEM_BYTES),
    )(swapped.reshape(1), parts, level_input, gain)


def join_kernel(swapped_ref, blocks_ref, out_ref):
    cols = blocks_ref.shape[2]
    own = cols // SIDE

    @pl.when(swapped_ref[0] == 0)
    def _():
        for j in range(SIDE):
            out_ref[:, j * cols : (j + 1) * cols] = blocks_ref[j]

    @pl.when(swapped_ref[0] == 1)
    def _():
        for j in range(SIDE):
            for k in range(SIDE):
                at = (k * SIDE + j) * own
                out_ref[:, at : at + own] = blocks_ref[j, :, k * own : (k + 1) * own]


def joined(swapped, blocks):
    side, own, cols = blocks.shape
    return pl.pallas_call(
        join_kernel,
        in_specs=[pl.BlockSpec(memory_space=pltpu.SMEM), pl.BlockSpec(memory_space=pltpu.VMEM)],
        out_shape=jax.ShapeDtypeStruct((own, side * cols), bf16),
        compiler_params=pltpu.CompilerParams(vmem_limit_bytes=VMEM_BYTES),
    )(swapped.reshape(1), blocks)


def axis_groups(sections):
    along, across = [], []
    for section in range(sections):
        base = section * SIDE * SIDE
        z_lines = [[base + z * SIDE + y for z in range(SIDE)] for y in range(SIDE)]
        y_lines = [[base + z * SIDE + y for y in range(SIDE)] for z in range(SIDE)]
        along += y_lines if section % 2 else z_lines
        across += z_lines if section % 2 else y_lines
    return along, across


def body(llm_grad, counts, offsets, owner, w_up, w_down, pre_act, fc1_input, level_input, ln_gain):
    z_index = lax.axis_index("z")
    y_index = lax.axis_index("y")
    device_index = z_index * SIDE + y_index
    section_index = lax.axis_index("section")
    swapped = (section_index % 2).astype(jnp.int32)
    along, across = axis_groups(lax.axis_size("section"))
    devices = ("section", "z", "y")

    def exchanged(blocks):
        return lax.all_to_all(blocks, devices, split_axis=0, concat_axis=0, axis_index_groups=along)

    micro_index = section_index // LEVELS
    level_index = section_index % LEVELS
    tok_count, width = llm_grad.shape[1:]
    slots = level_input.shape[1]
    images = counts.shape[1]
    rows = images * slots
    own = w_up.shape[1]
    merge = w_up.shape[2]
    chunk = width // REST

    down = w_down[0]
    shard, weight, down_tail = image_shard(
        llm_grad[0], w_up[0], down, micro_index, device_index, swapped, counts, offsets
    )
    gathered = lax.all_gather(shard.astype(f16), ("z", "y"), axis=0, tiled=True)

    owner_row = lax.dynamic_index_in_dim(owner, micro_index, 0, keepdims=False)
    number = jnp.arange(images, dtype=jnp.int32)
    slot = jnp.arange(slots, dtype=jnp.int32)[None, :]
    inverse = jnp.sum(jnp.where(owner_row[None, :] == number[:, None], number[None, :], 0), axis=1)
    source = (inverse[:, None] * slots + slot).reshape(1, rows).astype(jnp.int32)
    place = (owner_row[:, None] * slots + slot).reshape(rows)
    pre = pre_act[0].T
    gathered, weight, source, down_tail = lax.optimization_barrier((gathered, weight, source, down_tail))

    weight = exchanged(weight).reshape(SIDE * own, SIDE * own)
    power = gathered[:, width + chunk :].astype(f32)
    hidden_main = dot(gathered[:, :width].astype(bf16), down, ((1,), (1,)))
    hidden_tail = dot(
        gathered[:, width : width + chunk].astype(bf16), down_tail.reshape(REST * own, chunk), ((1,), (1,))
    )
    grad_pre, feed = hidden_gradient(source, power, hidden_main, hidden_tail, pre, fc1_input[0].T)
    weight, feed, grad_pre = lax.optimization_barrier((weight, feed, grad_pre))
    feed = exchanged(feed).reshape(SIDE * own, rows)
    panel = lax.all_gather(grad_pre.astype(f16), devices, axis=0, tiled=True, axis_index_groups=across)
    panel, feed = lax.optimization_barrier((panel, feed))

    def scaled_back(block):
        return (block[:, :rows].astype(f32) * jnp.exp2(-block[:, rows : rows + 1].astype(f32))).astype(bf16)

    parts = packed_rows(dot(scaled_back(panel), weight, ((0,), (1,))), images)
    parts, panel, feed, place, gathered, power = lax.optimization_barrier(
        (parts, panel, feed, place, gathered, power)
    )
    parts = lax.all_to_all(parts, ("z", "y"), split_axis=0, concat_axis=0)

    to_owner = (place[:, None] == jnp.arange(rows, dtype=jnp.int32)[None, :]).astype(bf16)
    feed = dot(feed, to_owner, ((1,), (0,))).astype(bf16)
    grad_up = dot(feed, scaled_back(panel), ((1,), (1,))).astype(bf16).reshape(SIDE, own, SIDE * own)
    act_main, act_tail = activations(power, pre)
    grad_down = dot(act_main, gathered[:, :width].astype(bf16), ((0,), (0,)))
    grad_down_tail = dot(act_tail, gathered[:, width : width + chunk].astype(bf16), ((0,), (0,)))
    grad_down_tail = grad_down_tail.reshape(REST, own, chunk).transpose(1, 0, 2).reshape(own, width)
    grad_down = (grad_down + grad_down_tail).astype(bf16)
    parts, grad_up, grad_down = lax.optimization_barrier((parts, grad_up, grad_down))

    grad_up = exchanged(grad_up)
    level_part = level_rows(swapped, parts, level_input[0], ln_gain)

    count = lax.axis_size("section")
    other = lax.ppermute(level_part, "section", [(source, source ^ 1) for source in range(count)])
    pair_sum = level_part + other
    below = [(source, source - 2) for source in range(count) if source % LEVELS >= 2]
    above = lax.ppermute(pair_sum.astype(bf16), "section", below)
    above, grad_up = lax.optimization_barrier((above, grad_up))
    grad_up = joined(swapped, grad_up)
    above = above.astype(f32)
    summed = jnp.where(level_index % 2 == 0, pair_sum, level_part)
    summed = summed + jnp.where(level_index < 2, above, 0.0)
    return (summed.astype(bf16)[None], grad_up[None], grad_down[None])


def solution(mesh):
    sections = mesh.devices.shape[0]
    cube = Mesh(mesh.devices.reshape(sections, SIDE, SIDE), ("section", "z", "y"))
    rows = P("section", ("z", "y"), None)
    cols = P("section", None, ("z", "y"))
    return jax.shard_map(
        body,
        mesh=cube,
        in_specs=(rows, P(), P(), P(), rows, rows, cols, cols, rows, P("section", None)),
        out_specs=(rows, rows, rows),
        check_vma=False,
    )
```

```python
import functools

import jax
import jax.numpy as jnp
from jax import lax
from jax.experimental import pallas as pl
from jax.experimental.pallas import tpu as pltpu
from jax.sharding import Mesh, PartitionSpec as P

inv_sqrt_two = 0.7071067811865476
inv_sqrt_two_pi = 0.3989422804014327
f32 = jnp.float32
bf16 = jnp.bfloat16
f16 = jnp.float16

SIDE = 8
LEVELS = 4
MAIN = 16
REST = 4
LANES = 128
VMEM_BYTES = 20 * 1024 * 1024
FULL = 32768.0
LEAST_POWER = -113
POWERS = (86, 64, 32, 16, 8, 4, 2, 1)


def gelu_parts(pre_float):
    cdf_part = 0.5 * (1.0 + jax.scipy.special.erf(pre_float * inv_sqrt_two))
    activated = pre_float * cdf_part
    slope = cdf_part + pre_float * jnp.exp(-0.5 * pre_float * pre_float) * inv_sqrt_two_pi
    return (activated, slope)


def norm_backward(level_rows, owned, gain):
    x_float = level_rows.astype(f32)
    row_mean = jnp.mean(x_float, axis=-1, keepdims=True)
    centred = x_float - row_mean
    variance = jnp.mean(centred * centred, axis=-1, keepdims=True)
    inv_std = 1.0 / jnp.sqrt(variance + 1e-06)
    normalised = centred * inv_std
    scaled = owned.astype(f32) * gain
    first_mean = jnp.mean(scaled, axis=-1, keepdims=True)
    second_mean = jnp.mean(scaled * normalised, axis=-1, keepdims=True)
    return inv_std * (scaled - first_mean - normalised * second_mean)


def dot(a, b, dims):
    return lax.dot_general(a, b, (dims, ((), ())), preferred_element_type=f32)


def block_power(block):
    largest = jnp.max(jnp.abs(block), axis=(0, 1), keepdims=True)
    scale = jnp.full_like(largest, 2.0**LEAST_POWER)
    power = jnp.full_like(largest, float(LEAST_POWER))
    for step in POWERS:
        fits = largest * (scale * 2.0**step) <= FULL
        scale = jnp.where(fits, scale * 2.0**step, scale)
        power = jnp.where(fits, power + float(step), power)
    return scale, power


def window_start(micro, device, tok_count, slots, offsets_ref):
    start = offsets_ref[micro, device] - device * tok_count
    start = jnp.minimum(jnp.maximum(start, 0), tok_count - slots)
    return start, jnp.minimum(lax.div(start, MAIN), tok_count // MAIN - 3)


def shard_kernel(tok_count, info_ref, counts_ref, offsets_ref, first_ref, second_ref, third_ref, weight_ref, down_ref, out_ref, cut_ref, down_cut_ref):
    cols = cut_ref.shape[2]
    own = cols // SIDE

    @pl.when(info_ref[2] == 0)
    def _():
        for j in range(SIDE):
            cut_ref[j] = weight_ref[:, j * cols : (j + 1) * cols]

    @pl.when(info_ref[2] == 1)
    def _():
        for j in range(SIDE):
            for k in range(SIDE):
                at = (k * SIDE + j) * own
                cut_ref[j, :, k * own : (k + 1) * own] = weight_ref[:, at : at + own]

    cols = down_cut_ref.shape[2]
    for j in range(REST):
        down_cut_ref[j] = down_ref[:, j * cols : (j + 1) * cols]
    micro, device = info_ref[0], info_ref[1]
    start, base = window_start(micro, device, tok_count, MAIN + REST, offsets_ref)
    delta = start - base * MAIN
    count = counts_ref[micro, device]
    width = first_ref.shape[1]
    chunk = width // REST
    block = jnp.concatenate(
        [first_ref[...].astype(f32), second_ref[...].astype(f32), third_ref[...].astype(f32)], axis=0
    )
    total = block.shape[0]
    block = pltpu.roll(block, lax.rem(total - delta, total), 0)[: MAIN + 2 * REST]
    slot = lax.broadcasted_iota(jnp.int32, block.shape, 0)
    block = jnp.where(slot < count, block, 0.0)
    scale, power = block_power(block)
    block = block * scale
    out_ref[:, :width] = block[:MAIN].astype(bf16)
    pieces = [block[MAIN:, c * chunk : (c + 1) * chunk] for c in range(REST)]
    upper = pieces[0] + pltpu.roll(pieces[1], REST, 0)
    lower = pieces[2] + pltpu.roll(pieces[3], REST, 0)
    out_ref[:, width : width + chunk] = jnp.concatenate([upper, lower], axis=0).astype(bf16)
    out_ref[:, width + chunk :] = jnp.broadcast_to(power, (MAIN, LANES)).astype(bf16)


def image_shard(rows, weight, down, micro, device, swapped, counts, offsets):
    tok_count, width = rows.shape
    own, merge = weight.shape
    info = jnp.stack([micro, device, swapped]).astype(jnp.int32)
    out_cols = width + width // REST + LANES

    def at(ahead):
        def index(step, info_ref, counts_ref, offsets_ref):
            return (window_start(info_ref[0], info_ref[1], tok_count, MAIN + REST, offsets_ref)[1] + ahead, 0)

        return pl.BlockSpec((MAIN, width), index)

    return pl.pallas_call(
        functools.partial(shard_kernel, tok_count),
        grid_spec=pltpu.PrefetchScalarGridSpec(
            num_scalar_prefetch=3,
            grid=(1,),
            in_specs=[
                at(0),
                at(1),
                at(2),
                pl.BlockSpec((own, merge), lambda step, *refs: (0, 0)),
                pl.BlockSpec((own, width), lambda step, *refs: (0, 0)),
            ],
            out_specs=[
                pl.BlockSpec((MAIN, out_cols), lambda step, *refs: (0, 0)),
                pl.BlockSpec((SIDE, own, merge // SIDE), lambda step, *refs: (0, 0, 0)),
                pl.BlockSpec((REST, own, width // REST), lambda step, *refs: (0, 0, 0)),
            ],
        ),
        out_shape=[
            jax.ShapeDtypeStruct((MAIN, out_cols), bf16),
            jax.ShapeDtypeStruct((SIDE, own, merge // SIDE), bf16),
            jax.ShapeDtypeStruct((REST, own, width // REST), bf16),
        ],
        compiler_params=pltpu.CompilerParams(vmem_limit_bytes=3 * VMEM_BYTES),
    )(info, counts, offsets, rows, rows, rows, weight, down)


def hidden_kernel(source_ref, power_ref, main_ref, tail_ref, pre_ref, feed_ref, out_ref, copies_ref, image_rows):
    for j in range(SIDE):
        copies_ref[j] = feed_ref[...]
    main_rows, own = main_ref.shape
    rows = image_rows.shape[0]
    images = main_rows // MAIN
    slots = rows // images
    unscale = jnp.exp2(-power_ref[...])[:, :own]
    row = lax.broadcasted_iota(jnp.int32, (main_rows, own), 0)
    chunk = lax.rem(lax.div(row, REST), REST)
    tail = jnp.zeros((main_rows, own), f32)
    for c in range(REST):
        tail += jnp.where(chunk == c, tail_ref[:, c * own : (c + 1) * own], 0.0)
    tail = (tail * unscale).reshape(images, 2, 2 * REST, own)
    tail = (tail[:, 0] + tail[:, 1]).reshape(main_rows // 2, own)
    tail = tail + pltpu.roll(tail, main_rows // 2 - REST, 0)
    main = main_ref[...] * unscale
    image_rows[...] = jnp.zeros_like(image_rows)
    for i in range(images):
        image_rows[i * slots : i * slots + MAIN, :own] = main[i * MAIN : (i + 1) * MAIN]
        image_rows[i * slots + MAIN : (i + 1) * slots, :own] = tail[i * 2 * REST : i * 2 * REST + REST]
    slope = gelu_parts(pre_ref[...].astype(f32))[1]
    grad_pre = (image_rows[...].T[:own] * slope).astype(bf16)
    scale, power = block_power(grad_pre.astype(f32))
    index = lax.broadcasted_iota(jnp.int32, (rows, 2 * LANES), 0)
    for part in range(rows // (2 * LANES)):
        at = slice(part * 2 * LANES, (part + 1) * 2 * LANES)
        order = jnp.where(index == source_ref[:, at], 1.0, 0.0).astype(bf16)
        out_ref[:, at] = (jnp.dot(grad_pre, order, preferred_element_type=f32) * scale).astype(bf16)
    out_ref[:, rows:] = jnp.broadcast_to(power, (own, LANES)).astype(bf16)


def hidden_gradient(source, power, main, tail, pre, feed):
    own, rows = pre.shape
    return pl.pallas_call(
        hidden_kernel,
        out_shape=[
            jax.ShapeDtypeStruct((own, rows + LANES), bf16),
            jax.ShapeDtypeStruct((SIDE, own, rows), bf16),
        ],
        scratch_shapes=[pltpu.VMEM((rows, LANES), f32)],
        compiler_params=pltpu.CompilerParams(vmem_limit_bytes=VMEM_BYTES),
    )(source, power, main, tail, pre, feed)


def activation_kernel(power_ref, pre_ref, main_ref, tail_ref, image_rows, spread):
    main_rows, own = main_ref.shape
    rows = image_rows.shape[0]
    images = main_rows // MAIN
    slots = rows // images
    unscale = jnp.exp2(-power_ref[...])
    activated = gelu_parts(pre_ref[...].astype(f32))[0].astype(bf16).astype(f32)
    pad = jnp.zeros((LANES - own, rows), f32)
    image_rows[...] = jnp.concatenate([activated, pad], axis=0).T
    for i in range(images):
        spread[i * MAIN : (i + 1) * MAIN, :] = image_rows[i * slots : i * slots + MAIN, :]
    main_ref[...] = (spread[...] * unscale)[:, :own].astype(bf16)
    for i in range(images):
        for c in range(REST):
            at = i * MAIN + c * REST
            spread[at : at + REST, :] = image_rows[i * slots + MAIN : (i + 1) * slots, :]
    tail = (spread[...] * unscale)[:, :own]
    row = lax.broadcasted_iota(jnp.int32, (main_rows, own), 0)
    chunk = lax.rem(lax.div(row, REST), REST)
    for c in range(REST):
        tail_ref[:, c * own : (c + 1) * own] = jnp.where(chunk == c, tail, 0.0).astype(bf16)


def activations(power, pre):
    own, rows = pre.shape
    main_rows = power.shape[0]
    return pl.pallas_call(
        activation_kernel,
        out_shape=[
            jax.ShapeDtypeStruct((main_rows, own), bf16),
            jax.ShapeDtypeStruct((main_rows, REST * own), bf16),
        ],
        scratch_shapes=[pltpu.VMEM((rows, LANES), f32), pltpu.VMEM((main_rows, LANES), f32)],
        compiler_params=pltpu.CompilerParams(vmem_limit_bytes=VMEM_BYTES),
    )(power, pre)


def pack_kernel(rows_ref, out_ref, packed):
    images = out_ref.shape[0]
    slots = rows_ref.shape[0] // images
    whole = rows_ref.shape[1] // LANES
    rest = rows_ref.shape[1] - whole * LANES
    packed[...] = jnp.zeros_like(packed)
    for i in range(images):
        block = rows_ref[i * slots : (i + 1) * slots, :]
        for c in range(whole):
            packed[i, c * slots : (c + 1) * slots, :] = block[:, c * LANES : (c + 1) * LANES]
        at = slice(whole * slots, whole * slots + slots // 2)
        packed[i, at, :rest] = block[: slots // 2, whole * LANES :]
        packed[i, at, rest:] = block[slots // 2 :, whole * LANES :]
    out_ref[...] = packed[...].astype(bf16)


def packed_rows(rows, images):
    slots = rows.shape[0] // images
    height = -(-slots * rows.shape[1] // LANES // MAIN) * MAIN
    return pl.pallas_call(
        pack_kernel,
        out_shape=jax.ShapeDtypeStruct((images, height, LANES), bf16),
        scratch_shapes=[pltpu.VMEM((images, height, LANES), f32)],
        compiler_params=pltpu.CompilerParams(vmem_limit_bytes=VMEM_BYTES),
    )(rows)


def level_kernel(swapped_ref, parts_ref, level_ref, gain_ref, out_ref, sums, owned):
    slots, merge = level_ref.shape
    cols = merge // SIDE
    own = cols // SIDE
    whole = cols // LANES
    rest = cols - whole * LANES

    def summed(sources):
        total = parts_ref[sources[0]].astype(f32)
        for source in sources[1:]:
            total = total + parts_ref[source].astype(f32)
        sums[...] = total
        pieces = [sums[c * slots : (c + 1) * slots, :] for c in range(whole)]
        last = sums[whole * slots : whole * slots + slots // 2, :]
        pieces.append(jnp.concatenate([last[:, :rest], last[:, rest:]], axis=0))
        return jnp.concatenate(pieces, axis=1)

    @pl.when(swapped_ref[0] == 0)
    def _():
        for y in range(SIDE):
            block = summed([z * SIDE + y for z in range(SIDE)])
            for z in range(SIDE):
                at = (z * SIDE + y) * own
                owned[:, at : at + own] = block[:, z * own : (z + 1) * own]

    @pl.when(swapped_ref[0] == 1)
    def _():
        for z in range(SIDE):
            owned[:, z * cols : (z + 1) * cols] = summed([z * SIDE + y for y in range(SIDE)])

    out_ref[...] = norm_backward(level_ref[...], owned[...], gain_ref[...])


def level_rows(swapped, parts, level_input, gain):
    slots, merge = level_input.shape
    vmem = pl.BlockSpec(memory_space=pltpu.VMEM)
    return pl.pallas_call(
        level_kernel,
        in_specs=[pl.BlockSpec(memory_space=pltpu.SMEM), vmem, vmem, vmem],
        out_shape=jax.ShapeDtypeStruct((slots, merge), f32),
        scratch_shapes=[pltpu.VMEM(parts.shape[1:], f32), pltpu.VMEM((slots, merge), f32)],
        compiler_params=pltpu.CompilerParams(vmem_limit_bytes=VMEM_BYTES),
    )(swapped.reshape(1), parts, level_input, gain)


def join_kernel(swapped_ref, blocks_ref, part_ref, pair_ref, above_ref, out_ref, level_ref):
    lower, upper = swapped_ref[1] < 2, swapped_ref[0] == 1
    summed = jnp.where(upper, part_ref[...], pair_ref[...])
    level_ref[...] = (summed + jnp.where(lower, above_ref[...].astype(f32), 0.0)).astype(bf16)
    cols = blocks_ref.shape[2]
    own = cols // SIDE

    @pl.when(swapped_ref[0] == 0)
    def _():
        for j in range(SIDE):
            out_ref[:, j * cols : (j + 1) * cols] = blocks_ref[j]

    @pl.when(swapped_ref[0] == 1)
    def _():
        for j in range(SIDE):
            for k in range(SIDE):
                at = (k * SIDE + j) * own
                out_ref[:, at : at + own] = blocks_ref[j, :, k * own : (k + 1) * own]


def joined(swapped, level, blocks, part, pair, above):
    side, own, cols = blocks.shape
    vmem = pl.BlockSpec(memory_space=pltpu.VMEM)
    return pl.pallas_call(
        join_kernel,
        in_specs=[pl.BlockSpec(memory_space=pltpu.SMEM)] + [vmem] * 4,
        out_shape=[jax.ShapeDtypeStruct((own, side * cols), bf16), jax.ShapeDtypeStruct(part.shape, bf16)],
        compiler_params=pltpu.CompilerParams(vmem_limit_bytes=VMEM_BYTES),
    )(jnp.stack([swapped, level.astype(jnp.int32)]), blocks, part, pair, above)


def axis_groups(sections):
    along, across = [], []
    for section in range(sections):
        base = section * SIDE * SIDE
        z_lines = [[base + z * SIDE + y for z in range(SIDE)] for y in range(SIDE)]
        y_lines = [[base + z * SIDE + y for y in range(SIDE)] for z in range(SIDE)]
        along += y_lines if section % 2 else z_lines
        across += z_lines if section % 2 else y_lines
    return along, across


def body(llm_grad, counts, offsets, owner, w_up, w_down, pre_act, fc1_input, level_input, ln_gain):
    z_index = lax.axis_index("z")
    y_index = lax.axis_index("y")
    device_index = z_index * SIDE + y_index
    section_index = lax.axis_index("section")
    swapped = (section_index % 2).astype(jnp.int32)
    along, across = axis_groups(lax.axis_size("section"))
    devices = ("section", "z", "y")

    def exchanged(blocks):
        return lax.all_to_all(blocks, devices, split_axis=0, concat_axis=0, axis_index_groups=along)

    micro_index = section_index // LEVELS
    level_index = section_index % LEVELS
    tok_count, width = llm_grad.shape[1:]
    slots = level_input.shape[1]
    images = counts.shape[1]
    rows = images * slots
    own = w_up.shape[1]
    merge = w_up.shape[2]
    chunk = width // REST

    down = w_down[0]
    shard, weight, down_tail = image_shard(
        llm_grad[0], w_up[0], down, micro_index, device_index, swapped, counts, offsets
    )
    gathered = lax.all_gather(shard.astype(f16), ("z", "y"), axis=0, tiled=True)

    owner_row = lax.dynamic_index_in_dim(owner, micro_index, 0, keepdims=False)
    number = jnp.arange(images, dtype=jnp.int32)
    slot = jnp.arange(slots, dtype=jnp.int32)[None, :]
    inverse = jnp.sum(jnp.where(owner_row[None, :] == number[:, None], number[None, :], 0), axis=1)
    source = (inverse[:, None] * slots + slot).reshape(1, rows).astype(jnp.int32)
    place = (owner_row[:, None] * slots + slot).reshape(rows)
    pre = pre_act[0].T
    gathered, weight, source, down_tail = lax.optimization_barrier((gathered, weight, source, down_tail))

    weight = exchanged(weight).reshape(SIDE * own, SIDE * own)
    power = gathered[:, width + chunk :].astype(f32)
    hidden_main = dot(gathered[:, :width].astype(bf16), down, ((1,), (1,)))
    hidden_tail = dot(
        gathered[:, width : width + chunk].astype(bf16), down_tail.reshape(REST * own, chunk), ((1,), (1,))
    )
    grad_pre, feed = hidden_gradient(source, power, hidden_main, hidden_tail, pre, fc1_input[0].T)
    weight, feed, grad_pre = lax.optimization_barrier((weight, feed, grad_pre))
    feed = exchanged(feed).reshape(SIDE * own, rows)
    panel = lax.all_gather(grad_pre.astype(f16), devices, axis=0, tiled=True, axis_index_groups=across)
    panel, feed = lax.optimization_barrier((panel, feed))

    def scaled_back(block):
        return (block[:, :rows].astype(f32) * jnp.exp2(-block[:, rows : rows + 1].astype(f32))).astype(bf16)

    parts = packed_rows(dot(scaled_back(panel), weight, ((0,), (1,))), images)
    parts, panel, feed, place, gathered, power = lax.optimization_barrier(
        (parts, panel, feed, place, gathered, power)
    )
    parts = lax.all_to_all(parts, ("z", "y"), split_axis=0, concat_axis=0)

    to_owner = (place[:, None] == jnp.arange(rows, dtype=jnp.int32)[None, :]).astype(bf16)
    feed = dot(feed, to_owner, ((1,), (0,))).astype(bf16)
    grad_up = dot(feed, scaled_back(panel), ((1,), (1,))).astype(bf16).reshape(SIDE, own, SIDE * own)
    act_main, act_tail = activations(power, pre)
    grad_down = dot(act_main, gathered[:, :width].astype(bf16), ((0,), (0,)))
    grad_down_tail = dot(act_tail, gathered[:, width : width + chunk].astype(bf16), ((0,), (0,)))
    grad_down_tail = grad_down_tail.reshape(REST, own, chunk).transpose(1, 0, 2).reshape(own, width)
    grad_down = (grad_down + grad_down_tail).astype(bf16)
    parts, grad_up, grad_down = lax.optimization_barrier((parts, grad_up, grad_down))

    grad_up = exchanged(grad_up)
    level_part = level_rows(swapped, parts, level_input[0], ln_gain)

    count = lax.axis_size("section")
    other = lax.ppermute(level_part, "section", [(source, source ^ 1) for source in range(count)])
    pair_sum = level_part + other
    below = [(source, source - 2) for source in range(count) if source % LEVELS >= 2]
    above = lax.ppermute(pair_sum.astype(bf16), "section", below)
    grad_up, summed = joined(swapped, level_index, grad_up, level_part, pair_sum, above)
    return (summed[None], grad_up[None], grad_down[None])


def solution(mesh):
    sections = mesh.devices.shape[0]
    cube = Mesh(mesh.devices.reshape(sections, SIDE, SIDE), ("section", "z", "y"))
    rows = P("section", ("z", "y"), None)
    cols = P("section", None, ("z", "y"))
    return jax.shard_map(
        body,
        mesh=cube,
        in_specs=(rows, P(), P(), P(), rows, rows, cols, cols, rows, P("section", None)),
        out_specs=(rows, rows, rows),
        check_vma=False,
    )
```
